32 devices in a mesh: fsdp: 4 (over y, x), tensor: 8 (over z, core).
Axes of the slice: x: 2, y: 2, z: 4, core: 2. Of those that a mesh axis runs over, the one named last changes fastest.
Arguments:
- inputs: bfloat16 [16, 729, 1152], P('fsdp'), may hold values from -6 to 6
- cotangent: bfloat16 [16, 729, 1152], P('fsdp'), may hold values from -6 to 6
- qkv_proj: bfloat16 [1152, 16, 216], P('fsdp', 'tensor'), may hold values from -0.1875 to 0.1875
- qv_bias: bfloat16 [16, 144], P('tensor'), may hold values from -3 to 3
- out_proj: bfloat16 [16, 72, 1152], P('tensor', None, 'fsdp'), may hold values from -3 to 3
- out_bias: bfloat16 [1152], P('fsdp'), may hold values from -3 to 3
- gain_one: bfloat16 [1152], P('fsdp'), may hold values from 0.099609375 to 1.8984375
- shift_one: bfloat16 [1152], P('fsdp'), may hold values from -3 to 3
- gain_two: bfloat16 [1152], P('fsdp'), may hold values from 0.099609375 to 1.8984375
- shift_two: bfloat16 [1152], P('fsdp'), may hold values from -3 to 3
- up_proj: bfloat16 [1152, 4304], P('fsdp', 'tensor'), may hold values from -0.1875 to 0.1875
- up_bias: bfloat16 [4304], P('tensor'), may hold values from -3 to 3
- down_proj: bfloat16 [4304, 1152], P('tensor', 'fsdp'), may hold values from -0.09375 to 0.09375
- down_bias: bfloat16 [1152], P('fsdp'), may hold values from -3 to 3
Outputs:
- layer_out: bfloat16 [16, 729, 1152], P('fsdp', None, 'tensor')
- input_gradient: float32 [16, 729, 1152], P('fsdp', None, 'tensor')
- qkv_grad: float32 [1152, 16, 216], P('fsdp', 'tensor')
- qvbias_grad: float32 [16, 144], P('tensor')
- outproj_grad: float32 [16, 72, 1152], P('tensor', None, 'fsdp')
- outbias_grad: float32 [1152], P('fsdp')
- gainone_grad: float32 [1152], P('fsdp')
- shiftone_grad: float32 [1152], P('fsdp')
- gaintwo_grad: float32 [1152], P('fsdp')
- shifttwo_grad: float32 [1152], P('fsdp')
- upproj_grad: float32 [1152, 4304], P('fsdp', 'tensor')
- upbias_grad: float32 [4304], P('tensor')
- downproj_grad: float32 [4304, 1152], P('tensor', 'fsdp')
- downbias_grad: float32 [1152], P('fsdp')
The draws below stay inside these ranges and needn't reach their ends.
All inputs are finite; a program needn't handle non-finite values.
Results may differ from the reference program's by a relative error of at most 0.024.
Values may be sent and summed in bfloat16 or wider, within the bound.
No kernel may reach another device: no remote copies, remote signals or barrier semaphores. Data moves between devices by JAX's collectives and lax.ppermute only.
A program may use at most 192 MiB of HBM per device.

```python
import jax
import jax.numpy as jnp
from jax import lax

MODEL_WIDTH = 1152
HEADS = 16
HD = 72
FF = 4304
SEQ = 729
IMAGES = 16


def level_of(stream_key, shape, pieces, least, top_value):
    def one(position, blocks):
        steps = jax.random.uniform(jax.random.fold_in(jax.random.fold_in(stream_key, 6), position), (blocks,), jnp.float32, least / len(pieces), top_value / len(pieces))
        return jnp.repeat(jnp.exp(steps), shape[position] // blocks).reshape((-1,) + (1,) * (len(shape) - position - 1))

    factor_of = one(*pieces[0])
    for cut in pieces[1:]:
        factor_of = factor_of * one(*cut)
    return factor_of


def bell_draw(stream_key, dims, spread, limit, cuts=(), held_as=jnp.bfloat16):
    entries = jax.random.normal(stream_key, dims, jnp.float32) * spread
    if len(cuts) > 0:
        entries = level_of(stream_key, dims, cuts, -0.22, 0.18) * entries
    return jnp.clip(entries, min=-limit, max=limit).astype(held_as)


def setup_inputs(seed: int = 0) -> dict:
    arg_keys = jax.random.split(jax.random.key(seed), 15)
    return {
        "inputs": bell_draw(arg_keys[0], (IMAGES, SEQ, MODEL_WIDTH), 1.0, 6.0, ((0, 4),)),
        "cotangent": bell_draw(arg_keys[1], (IMAGES, SEQ, MODEL_WIDTH), 1.0, 6.0, ((0, 4),)),
        "qkv_proj": bell_draw(arg_keys[2], (MODEL_WIDTH, HEADS, 3 * HD), MODEL_WIDTH ** -0.5, 0.1875, ((0, 4), (1, 8))),
        "qv_bias": bell_draw(arg_keys[3], (HEADS, 2 * HD), 0.5, 3.0, ((0, 8),)),
        "out_proj": bell_draw(arg_keys[4], (HEADS, HD, MODEL_WIDTH), (max(MODEL_WIDTH // 288, 1)) ** -0.5, 3.0, ((0, 8), (2, 4))),
        "out_bias": bell_draw(arg_keys[5], (MODEL_WIDTH,), 0.5, 3.0, ((0, 4),)),
        "gain_one": jnp.clip(1.0 + 0.18 * jax.random.normal(arg_keys[6], (MODEL_WIDTH,), jnp.float32), 0.099609375, 1.8984375).astype(jnp.bfloat16),
        "shift_one": bell_draw(arg_keys[7], (MODEL_WIDTH,), 0.5, 3.0, ((0, 4),)),
        "gain_two": jnp.clip(1.0 + 0.18 * jax.random.normal(arg_keys[8], (MODEL_WIDTH,), jnp.float32), 0.099609375, 1.8984375).astype(jnp.bfloat16),
        "shift_two": bell_draw(arg_keys[9], (MODEL_WIDTH,), 0.5, 3.0, ((0, 4),)),
        "up_proj": bell_draw(arg_keys[10], (MODEL_WIDTH, FF), MODEL_WIDTH ** -0.5, 0.1875, ((0, 4), (1, 8))),
        "up_bias": bell_draw(arg_keys[11], (FF,), 0.5, 3.0, ((0, 8),)),
        "down_proj": bell_draw(arg_keys[12], (FF, MODEL_WIDTH), FF ** -0.5, 0.09375, ((0, 8), (1, 4))),
        "down_bias": bell_draw(arg_keys[13], (MODEL_WIDTH,), 0.5, 3.0, ((0, 4),)),
    }


@jax.custom_vjp
def low(v):
    return lax.optimization_barrier(v.astype(jnp.bfloat16)).astype(jnp.float32)

@jax.custom_vjp
def low_back(v):
    return v

def low_keep(v):
    return (low(v), None)

def low_pass(kept, grad):
    return (grad,)

def back_keep(v):
    return (v, None)

def back_low(kept, grad):
    return (low(grad),)
low.defvjp(low_keep, low_pass)
low_back.defvjp(back_keep, back_low)
highest = lax.Precision.HIGHEST
norm_eps = 1e-06

def norm_rows(row_data, gain_vector, shift_vec):
    row_mean = lax.optimization_barrier(jnp.mean(row_data, axis=-1, keepdims=True))
    row_var = lax.optimization_barrier(jnp.mean(row_data * row_data, axis=-1, keepdims=True)) - row_mean * row_mean
    return (row_data - row_mean) * lax.rsqrt(row_var + norm_eps) * gain_vector + shift_vec

def round_both(values_in):
    return low_back(low(values_in))

def attend(triple):
    queries = round_both(triple[:, :, :HD])
    keys_rows = round_both(triple[:, :, HD:2 * HD])
    value_rows = round_both(triple[:, :, 2 * HD:])
    scores = low_back(jnp.einsum('qhe,khe->hqk', queries, keys_rows, precision=highest) * HD ** (-0.5))
    soft_probs = jax.nn.softmax(scores, axis=-1)
    context = jnp.einsum('hqk,khe->qhe', low(soft_probs), value_rows, precision=highest)
    return round_both(context)

def block_forward(inputs, qkv_proj, qv_bias, out_proj, out_bias, gain_one, shift_one, gain_two, shift_two, up_proj, up_bias, down_proj, down_bias):
    first_normed_rows = low(norm_rows(inputs, gain_one, shift_one))
    triple = jnp.einsum('bsd,dhe->bshe', first_normed_rows, qkv_proj, precision=highest)
    no_bias = jnp.zeros_like(qv_bias[:, :HD])
    full_bias = jnp.concatenate([qv_bias[:, :HD], no_bias, qv_bias[:, HD:]], axis=1)
    context = lax.map(jax.checkpoint(attend), triple + full_bias)
    branch = low_back(jnp.einsum('bshe,hed->bsd', context, out_proj, precision=highest))
    middle_residual = inputs + branch + out_bias
    normed_two = low(norm_rows(middle_residual, gain_two, shift_two))
    pre_act = low_back(jnp.einsum('bsd,df->bsf', normed_two, up_proj, precision=highest) + up_bias)
    hidden = low(jax.nn.gelu(pre_act, approximate=True))
    branch_two = low_back(jnp.einsum('bsf,fd->bsd', hidden, down_proj, precision=highest))
    return middle_residual + branch_two + down_bias

def reference(inputs, cotangent, qkv_proj, qv_bias, out_proj, out_bias, gain_one, shift_one, gain_two, shift_two, up_proj, up_bias, down_proj, down_bias):
    floats = [member.astype(jnp.float32) for member in (inputs, qkv_proj, qv_bias, out_proj, out_bias, gain_one, shift_one, gain_two, shift_two, up_proj, up_bias, down_proj, down_bias)]
    layer_out, pull_back = jax.vjp(block_forward, *floats)
    gradients = pull_back(cotangent.astype(jnp.float32))
    return (layer_out.astype(jnp.bfloat16), gradients[0], gradients[1], gradients[2], gradients[3], gradients[4], gradients[5], gradients[6], gradients[7], gradients[8], gradients[9], gradients[10], gradients[11], gradients[12])
```

```python
import functools

import jax
import jax.numpy as jnp
from jax import lax
from jax.experimental import pallas as pl
from jax.experimental.pallas import tpu as pltpu
from jax.sharding import PartitionSpec as P

HD = 72
norm_eps = 1e-06
LOG2E = 1.4426950408889634
bf16 = jnp.bfloat16
f32 = jnp.float32


def round_up(value, unit):
    return -(-value // unit) * unit


def nn(a, b):
    return lax.dot_general(a, b, (((1,), (0,)), ((), ())), preferred_element_type=f32)


def nt(a, b):
    return lax.dot_general(a, b, (((1,), (1,)), ((), ())), preferred_element_type=f32)


def fsdp_swap(x, bit):
    size = lax.axis_size("fsdp")
    return lax.ppermute(x, "fsdp", [(i, i ^ bit) for i in range(size)])


def tensor_swap(x, bit):
    size = lax.axis_size("tensor")
    return lax.ppermute(x, "tensor", [(i, i ^ bit) for i in range(size)])


def fsdp_bits(part):
    bits = []
    bit = 1
    while bit < lax.axis_size("fsdp"):
        bits.append(bit)
        bit *= 2
    return bits if part == 0 else bits[::-1]


def gather_rows(own):
    half = own.shape[1] // 2
    cut = lambda x, part: x[:, part * half : (part + 1) * half]
    first = {bit: fsdp_swap(own, bit) for bit in fsdp_bits(0)}
    pieces = []
    for part in (0, 1):
        have = {0: cut(own, part)}
        for bit in fsdp_bits(part):
            new = {}
            for offset, block in have.items():
                new[offset ^ bit] = cut(first[bit], part) if offset == 0 else fsdp_swap(block, bit)
            have.update(new)
        pieces += [have[o] for o in range(len(have))]
        used = half * len(have)
        spare = round_up(used, 128) - used
        if spare:
            pieces.append(jnp.zeros((own.shape[0], spare, own.shape[2]), own.dtype))
    return jnp.concatenate(pieces, axis=1)


def add_low(a, b):
    return (a.astype(f32) + b.astype(f32)).astype(bf16)


def split_blocks(x, axis, start, size):
    count = min(lax.axis_size("fsdp"), (x.shape[axis] - start) // size)
    return {n: lax.slice_in_dim(x, start + n * size, start + (n + 1) * size, axis=axis) for n in range(count)}


def scatter_rows(grads, rows):
    half_pad = grads.shape[1] // 2
    done = []
    for part in (0, 1):
        held = split_blocks(grads, 1, part * half_pad, rows // 2)
        for bit in fsdp_bits(part):
            leave = [o for o in held if o & bit]
            got = fsdp_swap(jnp.concatenate([held.pop(o) for o in leave], axis=1), bit)
            got = split_blocks(got, 1, 0, rows // 2)
            for n, o in enumerate(leave):
                held[o ^ bit] = add_low(held[o ^ bit], got[n])
        done.append(held[0])
    return jnp.concatenate(done, axis=1)


def attend_kernel(seq, heads, xn_ref, w_ref, bias_ref, qkv_ref, ctx_ref, lse_ref, part_ref, total):
    unit = pl.program_id(0)
    rows = xn_ref.shape[0]
    wide = heads * 3 * HD
    qkv = nn(xn_ref[...], w_ref[0, :, :wide]) + bias_ref[0]
    qkv_t = qkv.T
    qkv_ref[0] = qkv_t.astype(bf16)
    live = lax.broadcasted_iota(jnp.int32, (rows, 1), 0) < seq
    contexts = []
    for h in range(heads):
        at = h * 3 * HD
        q_t = qkv_t[at : at + HD].astype(bf16)
        k_n = qkv[:, at + HD : at + 2 * HD].astype(bf16)
        v_t = qkv_t[at + 2 * HD : at + 3 * HD].astype(bf16)
        scores = nn(k_n, q_t) * (HD**-0.5 * LOG2E)
        scores = jnp.where(live, scores, -1e30)
        top = jnp.max(scores, axis=0, keepdims=True)
        weight = jnp.exp2(scores - top)
        total_weight = jnp.sum(weight, axis=0, keepdims=True)
        lse_ref[0, h : h + 1, :] = top + jnp.log2(total_weight)
        contexts.append(nn(v_t, weight.astype(bf16)) / total_weight)
    ctx_t = jnp.concatenate(contexts, axis=0)
    ctx = ctx_t.T.astype(bf16)
    ctx_ref[0] = ctx
    add = nt(ctx, w_ref[0, :, wide : wide + heads * HD])

    @pl.when(unit == 0)
    def _():
        total[...] = add

    @pl.when(unit > 0)
    def _():
        total[...] += add

    @pl.when(unit == pl.num_programs(0) - 1)
    def _():
        half = total.shape[1] // 2
        part_ref[0] = total[:, :half].astype(bf16)
        part_ref[1] = total[:, half:].astype(bf16)


def attend(xn, weights, bias, seq, heads):
    units, feats, cols = weights.shape
    rows = xn.shape[0]
    wide = heads * 3 * HD
    return pl.pallas_call(
        functools.partial(attend_kernel, seq, heads),
        grid=(units,),
        in_specs=[
            pl.BlockSpec((rows, feats), lambda u: (0, 0)),
            pl.BlockSpec((1, feats, cols), lambda u: (u, 0, 0)),
            pl.BlockSpec((1, 1, wide), lambda u: (u, 0, 0)),
        ],
        out_specs=[
            pl.BlockSpec((1, wide, rows), lambda u: (u, 0, 0)),
            pl.BlockSpec((1, rows, heads * HD), lambda u: (u, 0, 0)),
            pl.BlockSpec((1, heads, rows), lambda u: (u, 0, 0)),
            pl.BlockSpec((2, rows, feats // 2), lambda u: (0, 0, 0)),
        ],
        out_shape=[
            jax.ShapeDtypeStruct((units, wide, rows), bf16),
            jax.ShapeDtypeStruct((units, rows, heads * HD), bf16),
            jax.ShapeDtypeStruct((units, heads, rows), f32),
            jax.ShapeDtypeStruct((2, rows, feats // 2), bf16),
        ],
        scratch_shapes=[pltpu.VMEM((rows, feats), f32)],
        compiler_params=pltpu.CompilerParams(vmem_limit_bytes=56 * 1024 * 1024),
        cost_estimate=pl.CostEstimate(
            flops=units * 2 * rows * (feats * cols + heads * 2 * rows * 256),
            bytes_accessed=2 * (units * feats * cols + 4 * rows * feats),
            transcendentals=units * heads * rows * rows,
        ),
    )(xn, weights, bias)


def attend_back_kernel(
    seq, heads, xnt_ref, bg_ref, bgt_ref, w_ref, qkv_ref, ctx_ref, lse_ref,
    dw_ref, db_ref, part_ref, total,
):
    unit = pl.program_id(0)
    rows = bg_ref.shape[0]
    wide = heads * 3 * HD
    d_ctx_t = nn(bg_ref[...], w_ref[0, :, wide : wide + heads * HD]).T
    qkv_t = qkv_ref[0].astype(f32)
    qkv = qkv_t.T
    live = lax.broadcasted_iota(jnp.int32, (rows, 1), 0) < seq
    scale = HD**-0.5
    pieces = []
    for h in range(heads):
        at = h * 3 * HD
        q_t = qkv_t[at : at + HD].astype(bf16)
        k_t = qkv_t[at + HD : at + 2 * HD].astype(bf16)
        k_n = qkv[:, at + HD : at + 2 * HD].astype(bf16)
        v_n = qkv[:, at + 2 * HD : at + 3 * HD].astype(bf16)
        d_o = d_ctx_t[h * HD : (h + 1) * HD].astype(bf16)
        scores = nn(k_n, q_t) * (scale * LOG2E)
        probs = jnp.where(live, jnp.exp2(scores - lse_ref[0, h : h + 1, :]), 0.0)
        d_probs = nn(v_n, d_o)
        delta = jnp.sum(d_probs * probs, axis=0, keepdims=True)
        d_scores = (probs * (d_probs - delta)).astype(bf16)
        d_v = nt(probs.astype(bf16), d_o)
        d_k = nt(d_scores, q_t) * scale
        d_q = nn(k_t, d_scores) * scale
        pieces += [d_q.T, d_k, d_v]
    d_qkv = jnp.concatenate(pieces, axis=1).astype(bf16)
    db_ref[0] = jnp.sum(d_qkv.astype(f32), axis=0, keepdims=True)
    dw_ref[0, :, :wide] = nn(xnt_ref[...], d_qkv).astype(bf16)
    dw_ref[0, :, wide : wide + heads * HD] = nn(bgt_ref[...], ctx_ref[0]).astype(bf16)
    add = nt(d_qkv, w_ref[0, :, :wide])

    @pl.when(unit == 0)
    def _():
        total[...] = add

    @pl.when(unit > 0)
    def _():
        total[...] += add

    @pl.when(unit == pl.num_programs(0) - 1)
    def _():
        half = total.shape[1] // 2
        part_ref[0] = total[:, :half].astype(bf16)
        part_ref[1] = total[:, half:].astype(bf16)


def attend_back(xnt, bg, bgt, weights, qkv_t, ctx, lse, seq, heads):
    units, feats, cols = weights.shape
    rows = bg.shape[0]
    wide = heads * 3 * HD
    by_unit = lambda *shape: pl.BlockSpec((1,) + shape, lambda u: (u, 0, 0))
    return pl.pallas_call(
        functools.partial(attend_back_kernel, seq, heads),
        grid=(units,),
        in_specs=[
            pl.BlockSpec((feats, rows), lambda u: (0, 0)),
            pl.BlockSpec((rows, feats), lambda u: (0, 0)),
            pl.BlockSpec((feats, rows), lambda u: (0, 0)),
            by_unit(feats, cols),
            by_unit(wide, rows),
            by_unit(rows, heads * HD),
            by_unit(heads, rows),
        ],
        out_specs=[
            by_unit(feats, cols),
            by_unit(1, wide),
            pl.BlockSpec((2, rows, feats // 2), lambda u: (0, 0, 0)),
        ],
        out_shape=[
            jax.ShapeDtypeStruct((units, feats, cols), bf16),
            jax.ShapeDtypeStruct((units, 1, wide), f32),
            jax.ShapeDtypeStruct((2, rows, feats // 2), bf16),
        ],
        scratch_shapes=[pltpu.VMEM((rows, feats), f32)],
        compiler_params=pltpu.CompilerParams(vmem_limit_bytes=56 * 1024 * 1024),
        cost_estimate=pl.CostEstimate(
            flops=units * 2 * rows * (2 * feats * cols + heads * 5 * rows * 256),
            bytes_accessed=2 * (2 * units * feats * cols + 6 * rows * feats),
            transcendentals=units * heads * rows * rows,
        ),
    )(xnt, bg, bgt, weights, qkv_t, ctx, lse)


def standardize(rows, width):
    mean = jnp.sum(rows, axis=-1, keepdims=True) / width
    var = jnp.sum(rows * rows, axis=-1, keepdims=True) / width - mean * mean
    rstd = lax.rsqrt(var + norm_eps)
    return (rows - mean) * rstd, rstd


def norm_back(grad, xhat, rstd, gain, width):
    a = grad * gain
    mean_a = jnp.sum(a, axis=-1, keepdims=True) / width
    mean_ax = jnp.sum(a * xhat, axis=-1, keepdims=True) / width
    return rstd * (a - mean_a - xhat * mean_ax)


def gelu_tanh(values_in):
    return jax.nn.gelu(values_in, approximate=True)


def body(
    inputs, cotangent, qkv_proj, qv_bias, out_proj, out_bias, gain_one, shift_one, gain_two,
    shift_two, up_proj, up_bias, down_proj, down_bias,
):
    fsdp, tensor = lax.axis_size("fsdp"), lax.axis_size("tensor")
    images, seq, width = inputs.shape
    groups = images
    sub = tensor // groups
    heads = qkv_proj.shape[1]
    units = up_proj.shape[1]
    shard = qkv_proj.shape[0]
    share = width // tensor
    half = shard // 2
    used = half * fsdp
    half_pad = round_up(used, 128)
    feats = 2 * half_pad
    rows = round_up(seq, 128)
    wide = heads * 3 * HD
    fi, ti = lax.axis_index("fsdp"), lax.axis_index("tensor")
    gi, ci = ti // sub, ti % 2
    group_bits = []
    bit = 1
    while bit < groups:
        group_bits.append(bit * sub)
        bit *= 2
    pair_bit, far_bits = group_bits[0], group_bits[1:][::-1]
    core_bits = []
    bit = 1
    while bit < sub:
        core_bits.append(bit)
        bit *= 2

    def gather_units(x, bits):
        for bit in bits:
            x = jnp.concatenate([x, tensor_swap(x, bit)], axis=0)
        return x

    def scatter_units(x, bits):
        for bit in bits[::-1]:
            keep = x.shape[0] // 2
            x = add_low(x[:keep], tensor_swap(x[keep:], bit))
        return x

    def swap_halves(x, axis):
        low = lax.slice_in_dim(x, 0, half, axis=axis)
        high = lax.slice_in_dim(x, half, 2 * half, axis=axis)
        a = jnp.where(ci == 0, low, high)
        b = jnp.where(ci == 0, high, low)
        return jnp.concatenate([a, b], axis=axis)

    feature_vectors = swap_halves(
        jnp.stack([out_bias, gain_one, shift_one, gain_two, shift_two, down_bias]), 1
    )
    unit_vectors = jnp.concatenate([qv_bias.reshape(-1), up_bias])[None]
    unit_vectors = gather_units(unit_vectors, far_bits + [pair_bit])
    vectors = gather_rows(feature_vectors[:, :, None])[:, :, 0].astype(f32)
    outb, gain1, shift1, gain2, shift2, downb = [vectors[i : i + 1] for i in range(6)]

    wire_a = jnp.concatenate(
        [qkv_proj.reshape(shard, wide), out_proj.reshape(heads * HD, shard).T], axis=1
    )
    wire_a = gather_units(swap_halves(wire_a, 0)[None], far_bits + [pair_bit])
    full_a = gather_rows(wire_a)
    wire_b = jnp.concatenate([up_proj, down_proj.T], axis=1)
    wire_b = gather_units(swap_halves(wire_b, 0)[None], far_bits)
    full_b = gather_rows(wire_b)
    unit_count = full_b.shape[0]
    bias_a = unit_vectors[:, : heads * 2 * HD].astype(f32).reshape(groups, heads, 2, HD)
    bias_a = jnp.concatenate(
        [bias_a[:, :, :1], jnp.zeros_like(bias_a[:, :, :1]), bias_a[:, :, 1:]], axis=2
    ).reshape(groups, 1, wide)
    bias_b = unit_vectors[:unit_count, heads * 2 * HD :].astype(f32)

    lane = jnp.arange(feats, dtype=jnp.int32)
    part, at = lane // half_pad, lane % half_pad
    block = jnp.minimum(at // half, fsdp - 1) ^ fi
    source = jnp.where(at < used, block * shard + (part ^ ci) * half + at % half, -1)
    place = (jnp.arange(width, dtype=jnp.int32)[:, None] == source[None, :]).astype(bf16)

    def arrange(x):
        x = jnp.pad(x, ((0, 0), (0, rows - seq), (0, 0)))
        return jnp.einsum("brd,de->bre", x, place, preferred_element_type=f32).astype(bf16)

    mine = lax.dynamic_slice_in_dim(inputs, gi, 1, 0)
    x = arrange(mine)[0].astype(f32)
    cot = arrange(
        jnp.concatenate(
            [
                lax.dynamic_slice_in_dim(cotangent, gi, 1, 0),
                lax.dynamic_slice_in_dim(cotangent, gi ^ 1, 1, 0),
            ]
        )
    )

    def sum_cores(parts):
        low, high = parts[0].astype(f32), parts[1].astype(f32)
        for bit in core_bits:
            other = tensor_swap(jnp.stack([low, high]).astype(bf16), bit).astype(f32)
            low, high = (low + other[1], high + other[0]) if bit == 1 else (low + other[0], high + other[1])
        return jnp.concatenate([low, high], axis=-1)

    def sum_pair(parts):
        low = parts.astype(bf16)
        low = add_low(low[..., :half_pad], tensor_swap(low[..., half_pad:], 1))
        for bit in core_bits[1:]:
            low = add_low(low, tensor_swap(low, bit))
        return low[0].astype(f32) + tensor_swap(low[1, :seq_pad], pair_bit).astype(f32)

    seq_pad = rows

    xhat1, rstd1 = standardize(x, width)
    xn = (xhat1 * gain1 + shift1).astype(bf16)
    qkv_t, ctx, lse, attn = attend(xn, full_a, bias_a, seq, heads)
    middle = x + sum_cores(attn) + outb
    xhat2, rstd2 = standardize(middle, width)
    n2 = (xhat2 * gain2 + shift2).astype(bf16)
    far_low = tensor_swap(n2[:, :half_pad], pair_bit)
    far_high = tensor_swap(far_low, 1)
    n2 = jnp.stack([n2, jnp.concatenate([far_low, far_high], axis=1)])
    up, down_t = full_b[:, :, :units], full_b[:, :, units:]
    pre_act = (
        jnp.einsum("brd,udf->burf", n2, up, preferred_element_type=f32) + bias_b[None, :, None]
    )
    hidden, pull = jax.vjp(gelu_tanh, pre_act)
    hidden = hidden.astype(bf16)
    mlp = jnp.einsum("burf,udf->brd", hidden, down_t, preferred_element_type=f32)
    out_half = middle[:, :half_pad] + sum_pair(mlp) + downb[:, :half_pad]

    cot_f = cot[0].astype(f32)
    downb_g = jnp.sum(cot_f, axis=0)
    hidden_grad = jnp.einsum("brd,udf->burf", cot, down_t, preferred_element_type=f32)
    pre_grad = pull(hidden_grad)[0].astype(bf16)
    up_bias_g = jnp.sum(pre_grad.astype(f32), axis=(0, 2))
    up_g = jnp.einsum("brd,burf->udf", n2, pre_grad, preferred_element_type=f32).astype(bf16)
    down_g = jnp.einsum("brd,burf->udf", cot, hidden, preferred_element_type=f32).astype(bf16)
    grad_b = scatter_rows(jnp.concatenate([up_g, down_g], axis=2), shard)
    grad_b = scatter_units(grad_b, far_bits)[0]
    n2_part = jnp.einsum("burf,udf->brd", pre_grad, up, preferred_element_type=f32)
    n2_low = sum_pair(n2_part)
    n2_high = tensor_swap(n2_low.astype(bf16), 1).astype(f32)
    n2_grad = jnp.concatenate([n2_low, n2_high], axis=1)
    gain2_g = jnp.sum(n2_grad * xhat2, axis=0)
    shift2_g = jnp.sum(n2_grad, axis=0)
    middle_grad = cot_f + norm_back(n2_grad, xhat2, rstd2, gain2, width)
    outb_g = jnp.sum(middle_grad, axis=0)
    branch_grad = middle_grad.astype(bf16)

    grad_a, bias_a_g, n1 = attend_back(
        xn.T, branch_grad, branch_grad.T, full_a, qkv_t, ctx, lse, seq, heads
    )
    grad_a = scatter_rows(grad_a, shard)
    grad_a = scatter_units(grad_a, far_bits + [pair_bit])[0]
    n1_grad = sum_cores(n1)
    gain1_g = jnp.sum(n1_grad * xhat1, axis=0)
    shift1_g = jnp.sum(n1_grad, axis=0)
    in_half = (middle_grad + norm_back(n1_grad, xhat1, rstd1, gain1, width))[:, :half_pad]

    def spread(y):
        y = y.astype(bf16)
        got = []
        for i in range(groups):
            first = ((gi ^ i) * sub + ti % sub) * share
            pick = (source[:half_pad, None] == first + jnp.arange(share, dtype=jnp.int32)[None]).astype(bf16)
            block = lax.dot_general(pick, y, (((0,), (1,)), ((), ())), preferred_element_type=f32).astype(bf16)
            got.append(tensor_swap(block, i * sub) if i else block)
        got = jnp.stack(got)
        for i, bit in enumerate(group_bits):
            paired = got.reshape((-1, 2, 1 << i) + got.shape[1:])
            paired = jnp.where((gi >> i) & 1 == 1, paired[:, ::-1], paired)
            got = paired.reshape(got.shape)
        return got.transpose(0, 2, 1)[:, :seq]

    layer_out = spread(out_half)
    input_grad = spread(in_half).astype(f32)

    vector_g = jnp.stack([outb_g, gain1_g, shift1_g, gain2_g, shift2_g, downb_g])
    for bit in group_bits:
        vector_g = vector_g + tensor_swap(vector_g, bit)
    vector_g = scatter_rows_exact(vector_g, shard)
    vector_g = swap_halves(vector_g, 1)
    qv_g = bias_a_g.reshape(groups, heads, 3, HD)[:, :, ::2].reshape(groups, heads * 2 * HD)
    for bit in (far_bits + [pair_bit])[::-1]:
        keep = qv_g.shape[0] // 2
        qv_g = qv_g[:keep] + tensor_swap(qv_g[keep:], bit)
    for bit in far_bits[::-1]:
        keep = up_bias_g.shape[0] // 2
        up_bias_g = up_bias_g[:keep] + tensor_swap(up_bias_g[keep:], bit)
    unit_g = jnp.concatenate([qv_g[0], up_bias_g[0]])[None]
    for bit in fsdp_bits(0):
        unit_g = unit_g + fsdp_swap(unit_g, bit)
    qvbias_g = unit_g[0, : heads * 2 * HD].reshape(heads, 2 * HD)
    upbias_g = unit_g[0, heads * 2 * HD :]

    grad_a = swap_halves(grad_a.astype(f32), 0)
    grad_b = swap_halves(grad_b.astype(f32), 0)
    return (
        layer_out,
        input_grad,
        grad_a[:, :wide].reshape(shard, heads, 3 * HD),
        qvbias_g,
        grad_a[:, wide:].T.reshape(heads, HD, shard),
        vector_g[0],
        vector_g[1],
        vector_g[2],
        vector_g[3],
        vector_g[4],
        grad_b[:, :units],
        upbias_g,
        grad_b[:, units:].T,
        vector_g[5],
    )


def scatter_rows_exact(vectors, rows):
    half_pad = vectors.shape[1] // 2
    done = []
    for part in (0, 1):
        held = split_blocks(vectors, 1, part * half_pad, rows // 2)
        for bit in fsdp_bits(part):
            leave = [o for o in held if o & bit]
            got = fsdp_swap(jnp.concatenate([held.pop(o) for o in leave], axis=1), bit)
            got = split_blocks(got, 1, 0, rows // 2)
            for n, o in enumerate(leave):
                held[o ^ bit] = held[o ^ bit] + got[n]
        done.append(held[0])
    return jnp.concatenate(done, axis=1)


def solution(mesh):
    return jax.shard_map(
        body,
        mesh=mesh,
        in_specs=(
            P("fsdp", None, None),
            P("fsdp", None, None),
            P("fsdp", "tensor", None),
            P("tensor", None),
            P("tensor", None, "fsdp"),
            P("fsdp"),
            P("fsdp"),
            P("fsdp"),
            P("fsdp"),
            P("fsdp"),
            P("fsdp", "tensor"),
            P("tensor"),
            P("tensor", "fsdp"),
            P("fsdp"),
        ),
        out_specs=(
            P("fsdp", None, "tensor"),
            P("fsdp", None, "tensor"),
            P("fsdp", "tensor", None),
            P("tensor", None),
            P("tensor", None, "fsdp"),
            P("fsdp"),
            P("fsdp"),
            P("fsdp"),
            P("fsdp"),
            P("fsdp"),
            P("fsdp", "tensor"),
            P("tensor"),
            P("tensor", "fsdp"),
            P("fsdp"),
        ),
        check_vma=False,
    )
```

```python
import functools

import jax
import jax.numpy as jnp
from jax import lax
from jax.experimental import pallas as pl
from jax.experimental.pallas import tpu as pltpu
from jax.sharding import PartitionSpec as P

HD = 72
norm_eps = 1e-06
LOG2E = 1.4426950408889634
GELU_A = 0.7978845608028654
GELU_B = 0.044715
MIB = 1024 * 1024
bf16 = jnp.bfloat16
f32 = jnp.float32


def round_up(value, unit):
    return -(-value // unit) * unit


def nn(a, b):
    return lax.dot_general(a, b, (((1,), (0,)), ((), ())), preferred_element_type=f32)


def nt(a, b):
    return lax.dot_general(a, b, (((1,), (1,)), ((), ())), preferred_element_type=f32)


def shaped(shape, dtype):
    return jax.ShapeDtypeStruct(shape, dtype)


def on_chip(kernel, out_shape, args, scratch=(), flops=0, exps=0):
    whole = pl.BlockSpec(memory_space=pltpu.VMEM)
    moved = sum(a.size * a.dtype.itemsize for a in list(args) + list(out_shape))
    return pl.pallas_call(
        kernel,
        in_specs=[whole] * len(args),
        out_specs=[whole] * len(out_shape),
        out_shape=list(out_shape),
        scratch_shapes=list(scratch),
        compiler_params=pltpu.CompilerParams(vmem_limit_bytes=60 * MIB),
        cost_estimate=pl.CostEstimate(flops=flops, bytes_accessed=moved, transcendentals=exps),
    )(*args)


def fsdp_swap(x, bit):
    size = lax.axis_size("fsdp")
    return lax.ppermute(x, "fsdp", [(i, i ^ bit) for i in range(size)])


def tensor_swap(x, bit):
    size = lax.axis_size("tensor")
    return lax.ppermute(x, "tensor", [(i, i ^ bit) for i in range(size)])


def fsdp_bits(part):
    bits = []
    bit = 1
    while bit < lax.axis_size("fsdp"):
        bits.append(bit)
        bit *= 2
    return bits if part == 0 else bits[::-1]


def gather_pieces(own):
    half = own.shape[0] // 2
    arrays = [own]
    first = {}
    for bit in fsdp_bits(0):
        first[bit] = len(arrays)
        arrays.append(fsdp_swap(own, bit))
    plan = []
    for part in (0, 1):
        have = {0: (0, part * half)}
        for bit in fsdp_bits(part):
            new = {}
            for offset, (index, row) in have.items():
                if offset == 0:
                    new[bit] = (first[bit], part * half)
                else:
                    new[offset ^ bit] = (len(arrays), 0)
                    arrays.append(fsdp_swap(arrays[index][row : row + half], bit))
            have.update(new)
        plan.append([have[o] for o in range(len(have))])
    return arrays, plan


def assemble(out, refs, plan, half, half_pad):
    for part in (0, 1):
        for offset, (index, row) in enumerate(plan[part]):
            at = part * half_pad + offset * half
            out[at : at + half, :] = refs[index][row : row + half, :]
        used = len(plan[part]) * half
        if used < half_pad:
            out[part * half_pad + used : (part + 1) * half_pad, :] = jnp.zeros(
                (half_pad - used, out.shape[1]), out.dtype
            )


def add_low(a, b):
    return (a.astype(f32) + b.astype(f32)).astype(bf16)


def split_blocks(x, axis, start, size):
    return {
        n: lax.slice_in_dim(x, start + n * size, start + (n + 1) * size, axis=axis)
        for n in range(lax.axis_size("fsdp"))
    }


def scatter_rows(grads, rows):
    done = []
    for part in (0, 1):
        held = split_blocks(grads, 0, part * (grads.shape[0] // 2), rows // 2)
        for bit in fsdp_bits(part):
            leave = [o for o in held if o & bit]
            got = fsdp_swap(jnp.concatenate([held.pop(o) for o in leave], axis=0), bit)
            for n, o in enumerate(leave):
                held[o ^ bit] = add_low(held[o ^ bit], got[n * (rows // 2) : (n + 1) * (rows // 2)])
        done.append(held[0])
    return jnp.concatenate(done, axis=0)


def attend_kernel(seq, heads, plan, count, first, *refs):
    xn_ref, bias_ref = refs[:2]
    pieces = refs[2 : 2 + count]
    rest = refs[2 + count :]
    if first:
        w_ref, qkv_ref, ctx_ref, lse_ref, part_ref = rest
    else:
        before_ref, w_ref, qkv_ref, ctx_ref, lse_ref, part_ref = rest
    rows, feats = xn_ref.shape
    half = feats // 2
    wide = heads * 3 * HD
    assemble(w_ref, pieces, plan, pieces[0].shape[0] // 2, half)
    qkv = nn(xn_ref[...], w_ref[:, :wide]) + bias_ref[...]
    qkv_t = qkv.T
    qkv_ref[...] = qkv_t.astype(bf16)
    live = lax.broadcasted_iota(jnp.int32, (rows, 1), 0) < seq
    contexts = []
    for h in range(heads):
        at = h * 3 * HD
        q_t = qkv_t[at : at + HD].astype(bf16)
        k_n = qkv[:, at + HD : at + 2 * HD].astype(bf16)
        v_t = qkv_t[at + 2 * HD : at + 3 * HD].astype(bf16)
        scores = nn(k_n, q_t) * (HD**-0.5 * LOG2E)
        scores = jnp.where(live, scores, -1e30)
        top = jnp.max(scores, axis=0, keepdims=True)
        weight = jnp.exp2(scores - top)
        total_weight = jnp.sum(weight, axis=0, keepdims=True)
        lse_ref[h : h + 1, :] = top + jnp.log2(total_weight)
        contexts.append(nn(v_t, weight.astype(bf16)) / total_weight)
    ctx = jnp.concatenate(contexts, axis=0).T.astype(bf16)
    ctx_ref[...] = ctx
    for n in (0, 1):
        add = nt(ctx, w_ref[n * half : (n + 1) * half, wide : wide + heads * HD])
        if not first:
            add = add + before_ref[n].astype(f32)
        part_ref[n] = add.astype(bf16)


def attend(xn, bias, pieces, plan, before, seq, heads):
    rows, feats = xn.shape
    wide = heads * 3 * HD
    cols = pieces[0].shape[1]
    args = [xn, bias] + pieces + ([] if before is None else [before])
    return on_chip(
        functools.partial(attend_kernel, seq, heads, plan, len(pieces), before is None),
        [
            shaped((feats, cols), bf16),
            shaped((wide, rows), bf16),
            shaped((rows, heads * HD), bf16),
            shaped((heads, rows), f32),
            shaped((2, rows, feats // 2), bf16),
        ],
        args,
        flops=2 * rows * (feats * cols + heads * 2 * rows * 256),
        exps=heads * rows * rows,
    )


def attend_back_kernel(seq, heads, first, *refs):
    xnt_ref, bg_ref, w_ref, qkv_ref, lse_ref = refs[:5]
    if first:
        dw_ref, db_ref, part_ref = refs[5:]
    else:
        before_ref, dw_ref, db_ref, part_ref = refs[5:]
    rows, feats = bg_ref.shape
    half = feats // 2
    wide = heads * 3 * HD
    d_ctx_t = nn(bg_ref[...], w_ref[:, wide : wide + heads * HD]).T
    qkv_t = qkv_ref[...].astype(f32)
    qkv = qkv_t.T
    live = lax.broadcasted_iota(jnp.int32, (rows, 1), 0) < seq
    scale = HD**-0.5
    pieces = []
    for h in range(heads):
        at = h * 3 * HD
        q_t = qkv_t[at : at + HD].astype(bf16)
        k_t = qkv_t[at + HD : at + 2 * HD].astype(bf16)
        k_n = qkv[:, at + HD : at + 2 * HD].astype(bf16)
        v_n = qkv[:, at + 2 * HD : at + 3 * HD].astype(bf16)
        d_o = d_ctx_t[h * HD : (h + 1) * HD].astype(bf16)
        scores = nn(k_n, q_t) * (scale * LOG2E)
        probs = jnp.where(live, jnp.exp2(scores - lse_ref[h : h + 1, :]), 0.0)
        d_probs = nn(v_n, d_o)
        delta = jnp.sum(d_probs * probs, axis=0, keepdims=True)
        d_scores = (probs * (d_probs - delta)).astype(bf16)
        d_v = nt(probs.astype(bf16), d_o)
        d_k = nt(d_scores, q_t) * scale
        d_q = nn(k_t, d_scores) * scale
        pieces += [d_q.T, d_k, d_v]
    d_qkv = jnp.concatenate(pieces, axis=1).astype(bf16)
    db_ref[...] = jnp.sum(d_qkv.astype(f32), axis=0, keepdims=True)
    dw_ref[...] = nn(xnt_ref[...], d_qkv).astype(bf16)
    for n in (0, 1):
        add = nt(d_qkv, w_ref[n * half : (n + 1) * half, :wide])
        if not first:
            add = add + before_ref[n].astype(f32)
        part_ref[n] = add.astype(bf16)


def attend_back(xnt, bg, weights, qkv_t, lse, before, seq, heads):
    rows, feats = bg.shape
    wide = heads * 3 * HD
    args = [xnt, bg, weights, qkv_t, lse] + ([] if before is None else [before])
    return on_chip(
        functools.partial(attend_back_kernel, seq, heads, before is None),
        [
            shaped((feats, wide), bf16),
            shaped((1, wide), f32),
            shaped((2, rows, feats // 2), bf16),
        ],
        args,
        flops=2 * rows * (2 * feats * wide + heads * 5 * rows * 256),
        exps=heads * rows * rows,
    )


def out_grad_kernel(count, bg_ref, *refs):
    ctx = jnp.concatenate([r[...].astype(f32) for r in refs[:count]], axis=1).astype(bf16)
    refs[count][...] = nn(bg_ref[...].astype(f32).T.astype(bf16), ctx).astype(bf16)


def out_grad(bg, contexts):
    rows, feats = bg.shape
    cols = sum(c.shape[1] for c in contexts)
    return on_chip(
        functools.partial(out_grad_kernel, len(contexts)),
        [shaped((feats, cols), bf16)],
        [bg] + contexts,
        flops=2 * rows * feats * cols,
    )[0]


def mlp_kernel(plan, counts, first, *refs):
    low_ref, high_ref, cot_ref, cott_ref, bias_ref = refs[:5]
    at = 5
    pieces = []
    for count in counts:
        pieces.append(refs[at : at + count])
        at += count
    before = []
    if not first:
        before = refs[at : at + len(counts)]
        at += len(counts)
    out_ref, back_ref, db_ref = refs[at : at + 3]
    dw_refs = refs[at + 3 : at + 3 + len(counts)]
    n2_ref, n2t_ref, w_ref, out_sum, back_sum = refs[at + 3 + len(counts) :]
    half = low_ref.shape[1]
    n2_ref[:, :half] = low_ref[...]
    n2_ref[:, half:] = high_ref[...]
    n2t_ref[:half, :] = low_ref[...].astype(f32).T.astype(bf16)
    n2t_ref[half:, :] = high_ref[...].astype(f32).T.astype(bf16)
    for u in range(len(counts)):
        assemble(w_ref, pieces[u], plan, pieces[u][0].shape[0] // 2, half)
        units = w_ref.shape[1] // 2
        up = w_ref[:, :units]
        down = w_ref[:, units:]
        v = nn(n2_ref[...], up) + bias_ref[u : u + 1, :]
        square = v * v
        t = jnp.tanh(GELU_A * v * (1.0 + GELU_B * square))
        hidden = (0.5 * v * (1.0 + t)).astype(bf16)
        slope = 0.5 * (1.0 + t) + (0.5 * GELU_A) * v * (1.0 - t * t) * (1.0 + 3.0 * GELU_B * square)
        pre_grad = (nn(cot_ref[...], down) * slope).astype(bf16)
        out_add = nt(hidden, down)
        back_add = nt(pre_grad, up)
        if u == 0:
            out_sum[...] = out_add
            back_sum[...] = back_add
        else:
            out_sum[...] += out_add
            back_sum[...] += back_add
        db_ref[u : u + 1, :] = jnp.sum(pre_grad.astype(f32), axis=0, keepdims=True)
        d_up = nn(n2t_ref[...], pre_grad)
        d_down = nn(cott_ref[...], hidden)
        if not first:
            d_up = d_up + before[u][:, :units].astype(f32)
            d_down = d_down + before[u][:, units:].astype(f32)
        dw_refs[u][:, :units] = d_up.astype(bf16)
        dw_refs[u][:, units:] = d_down.astype(bf16)
    for n in (0, 1):
        out_ref[n] = out_sum[:, n * half : (n + 1) * half].astype(bf16)
        back_ref[n] = back_sum[:, n * half : (n + 1) * half].astype(bf16)


def mlp(low, high, cot, cot_t, bias, gathered, before):
    rows, half = low.shape
    feats = 2 * half
    plan = gathered[0][1]
    cols = gathered[0][0][0].shape[1]
    args = [low, high, cot, cot_t, bias] + [a for g in gathered for a in g[0]] + list(before or [])
    found = on_chip(
        functools.partial(mlp_kernel, plan, [len(g[0]) for g in gathered], before is None),
        [
            shaped((2, rows, half), bf16),
            shaped((2, rows, half), bf16),
            shaped((len(gathered), cols // 2), f32),
        ]
        + [shaped((feats, cols), bf16)] * len(gathered),
        args,
        scratch=[
            pltpu.VMEM((rows, feats), bf16),
            pltpu.VMEM((feats, rows), bf16),
            pltpu.VMEM((feats, cols), bf16),
            pltpu.VMEM((rows, feats), f32),
            pltpu.VMEM((rows, feats), f32),
        ],
        flops=len(gathered) * 6 * rows * feats * cols,
        exps=len(gathered) * rows * cols // 2,
    )
    return found[0], found[1], found[2], found[3:]


def standardize(rows, width):
    mean = jnp.sum(rows, axis=-1, keepdims=True) / width
    var = jnp.sum(rows * rows, axis=-1, keepdims=True) / width - mean * mean
    rstd = lax.rsqrt(var + norm_eps)
    return (rows - mean) * rstd, rstd


def norm_back(grad, xhat, rstd, gain, width):
    a = grad * gain
    mean_a = jnp.sum(a, axis=-1, keepdims=True) / width
    mean_ax = jnp.sum(a * xhat, axis=-1, keepdims=True) / width
    return rstd * (a - mean_a - xhat * mean_ax)


def by_rows(kernel, out_shape, out_whole, args, whole, rows, tile):
    def spec(shape, uncut):
        if uncut:
            return pl.BlockSpec(shape, lambda i, n=len(shape): (0,) * n)
        if len(shape) == 3:
            return pl.BlockSpec((shape[0], tile, shape[2]), lambda i: (0, i, 0))
        return pl.BlockSpec((tile, shape[1]), lambda i: (i, 0))

    return pl.pallas_call(
        kernel,
        grid=(rows // tile,),
        in_specs=[spec(a.shape, w) for a, w in zip(args, whole)],
        out_specs=[spec(o.shape, w) for o, w in zip(out_shape, out_whole)],
        out_shape=list(out_shape),
        compiler_params=pltpu.CompilerParams(vmem_limit_bytes=40 * MIB),
        cost_estimate=pl.CostEstimate(
            flops=0,
            bytes_accessed=sum(a.size * a.dtype.itemsize for a in list(args) + list(out_shape)),
            transcendentals=0,
        ),
    )(*args)


def joined(ref):
    return jnp.concatenate([ref[0].astype(f32), ref[1].astype(f32)], axis=-1)


def crossed(ref):
    return jnp.concatenate([ref[1].astype(f32), ref[0].astype(f32)], axis=-1)


def middle_kernel(width, x_ref, own_ref, other_ref, vec_ref, middle_ref, low_ref, high_ref):
    half = low_ref.shape[1]
    middle = x_ref[...].astype(f32) + joined(own_ref) + crossed(other_ref) + vec_ref[0:1, :]
    middle_ref[...] = middle
    xhat, rstd = standardize(middle, width)
    n2 = (xhat * vec_ref[3:4, :] + vec_ref[4:5, :]).astype(bf16)
    low_ref[...] = n2[:, :half]
    high_ref[...] = n2[:, half:]


def add_sums(ref, sums):
    @pl.when(pl.program_id(0) == 0)
    def _():
        ref[...] = sums

    @pl.when(pl.program_id(0) > 0)
    def _():
        ref[...] += sums


def column_sums(parts):
    return jnp.concatenate([jnp.sum(p, axis=0, keepdims=True) for p in parts], axis=0)


def middle_back_kernel(width, low_ref, high_ref, middle_ref, cot_ref, vec_ref, grad_ref, bg_ref, sum_ref):
    half = low_ref.shape[1]
    grad = jnp.concatenate([low_ref[...].astype(f32), high_ref[...].astype(f32)], axis=-1)
    xhat, rstd = standardize(middle_ref[...], width)
    cot = cot_ref[...].astype(f32)
    back = cot + norm_back(grad, xhat, rstd, vec_ref[3:4, :], width)
    grad_ref[...] = back[:, :half]
    bg_ref[...] = back.astype(bf16)
    add_sums(
        sum_ref,
        column_sums([back[:, :half], grad[:, :half] * xhat[:, :half], grad[:, :half], cot[:, :half]]),
    )


def first_back_kernel(width, own_ref, other_ref, x_ref, grad_ref, vec_ref, pick_ref, out_ref, sum_ref):
    half = grad_ref.shape[1]
    grad = joined(own_ref) + crossed(other_ref)
    xhat, rstd = standardize(x_ref[...].astype(f32), width)
    back = norm_back(grad, xhat, rstd, vec_ref[1:2, :], width)
    result = (grad_ref[...] + back[:, :half]).astype(bf16)
    out_ref[...] = nt(pick_ref[...], result).astype(bf16)
    add_sums(sum_ref, column_sums([grad[:, :half] * xhat[:, :half], grad[:, :half]]))


def body(
    inputs, cotangent, qkv_proj, qv_bias, out_proj, out_bias, gain_one, shift_one, gain_two,
    shift_two, up_proj, up_bias, down_proj, down_bias,
):
    fsdp, tensor = lax.axis_size("fsdp"), lax.axis_size("tensor")
    images, seq, width = inputs.shape
    groups = images
    sub = tensor // groups
    heads = qkv_proj.shape[1]
    units = up_proj.shape[1]
    shard = qkv_proj.shape[0]
    share = width // tensor
    half = shard // 2
    used = half * fsdp
    half_pad = round_up(used, 128)
    feats = 2 * half_pad
    rows = round_up(seq, 128)
    tile = rows // 3 if rows % 384 == 0 else 128
    wide = heads * 3 * HD
    qv = heads * 2 * HD
    fi, ti = lax.axis_index("fsdp"), lax.axis_index("tensor")
    gi, ci = ti // sub, ti % 2
    group_bits = []
    bit = 1
    while bit < groups:
        group_bits.append(bit * sub)
        bit *= 2
    pair_bit, far_bits = group_bits[0], group_bits[1:][::-1]
    core_bits = []
    bit = 1
    while bit < sub:
        core_bits.append(bit)
        bit *= 2

    def gather_units(x, bits):
        have = [x]
        for bit in bits:
            have = have + [tensor_swap(h, bit) for h in have]
        return have

    def scatter_units(have, bits, add):
        for bit in bits[::-1]:
            keep = len(have) // 2
            have = [add(a, tensor_swap(b, bit)) for a, b in zip(have[:keep], have[keep:])]
        return have[0]

    def swap_halves(x, axis):
        low = lax.slice_in_dim(x, 0, half, axis=axis)
        high = lax.slice_in_dim(x, half, 2 * half, axis=axis)
        a = jnp.where(ci == 0, low, high)
        b = jnp.where(ci == 0, high, low)
        return jnp.concatenate([a, b], axis=axis)

    own_vectors = jnp.stack([out_bias, gain_one, shift_one, gain_two, shift_two, down_bias])
    own_vectors = swap_halves(own_vectors, 1)
    blocks = {0: own_vectors}
    for bit in fsdp_bits(0):
        blocks.update({o ^ bit: b for o, b in zip(blocks, fsdp_swap(jnp.stack(list(blocks.values())), bit))})
    spare = jnp.zeros((6, half_pad - used), bf16)
    vectors = jnp.concatenate(
        [blocks[o][:, :half] for o in range(fsdp)] + [spare]
        + [blocks[o][:, half:] for o in range(fsdp)] + [spare],
        axis=1,
    ).astype(f32)
    vectors = jnp.pad(vectors, ((0, 2), (0, 0)))
    unit_vectors = jnp.concatenate([qv_bias.reshape(-1), up_bias])[None]
    for bit in far_bits + [pair_bit]:
        unit_vectors = jnp.concatenate([unit_vectors, tensor_swap(unit_vectors, bit)])
    unit_vectors = unit_vectors.astype(f32)

    wire_a = jnp.concatenate(
        [qkv_proj.reshape(shard, wide), out_proj.reshape(heads * HD, shard).T], axis=1
    )
    wires_a = gather_units(swap_halves(wire_a, 0), far_bits + [pair_bit])
    wire_b = jnp.concatenate([up_proj, down_proj.T], axis=1)
    wires_b = gather_units(swap_halves(wire_b, 0), far_bits)
    order = sorted(range(groups), key=lambda u: (u != 0, u != groups // 2, u))
    gathered_a = {u: gather_pieces(wires_a[u]) for u in order}
    gathered_b = [gather_pieces(w) for w in wires_b]
    bias_a = unit_vectors[:, :qv].reshape(groups, heads, 2, HD)
    bias_a = jnp.concatenate(
        [bias_a[:, :, :1], jnp.zeros_like(bias_a[:, :, :1]), bias_a[:, :, 1:]], axis=2
    ).reshape(groups, 1, wide)
    bias_b = unit_vectors[: len(wires_b), qv:]

    lane = jnp.arange(feats, dtype=jnp.int32)
    part, at = lane // half_pad, lane % half_pad
    block = jnp.minimum(at // half, fsdp - 1) ^ fi
    source = jnp.where(at < used, block * shard + (part ^ ci) * half + at % half, -1)
    place = (jnp.arange(width, dtype=jnp.int32)[:, None] == source[None, :]).astype(bf16)

    def arrange(x, index):
        x = lax.dynamic_index_in_dim(x, index, 0, keepdims=False)
        x = jnp.pad(x, ((0, rows - seq), (0, 0)))
        return jnp.einsum("rd,de->re", x, place, preferred_element_type=f32).astype(bf16)

    x = arrange(inputs, gi)
    cots = [arrange(cotangent, gi), arrange(cotangent, gi ^ 1)]
    cots_t = [c.T for c in cots]
    out_share = jnp.arange(groups * share, dtype=jnp.int32)
    out_first = ((gi ^ (out_share // share)) * sub + ti % sub) * share + out_share % share
    pick = (out_first[:, None] == source[None, :half_pad]).astype(bf16)

    xhat1, _ = standardize(x.astype(f32), width)
    xn = (xhat1 * vectors[1:2] + vectors[2:3]).astype(bf16)
    xnt = xn.T
    kept = {}
    attn = None
    for u in order:
        arrays, plan = gathered_a[u]
        found = attend(xn, bias_a[u], arrays, plan, attn, seq, heads)
        kept[u] = found[:4]
        attn = found[4]

    def other_cores(parts):
        other = tensor_swap(parts, 1)
        for bit in core_bits[1:]:
            more = tensor_swap(jnp.stack([parts, other]), bit)
            parts, other = add_low(parts, more[0]), add_low(other, more[1])
        return parts, other

    attn, attn_other = other_cores(attn)
    middle, n2_low, n2_high = by_rows(
        functools.partial(middle_kernel, width),
        [shaped((rows, feats), f32), shaped((rows, half_pad), bf16), shaped((rows, half_pad), bf16)],
        [False] * 3,
        [x, attn, attn_other, vectors],
        [False, False, False, True],
        rows,
        tile,
    )
    far_low = tensor_swap(n2_low, pair_bit)
    far_high = tensor_swap(far_low, 1)

    out0, back0, up_bias0, dw0 = mlp(n2_low, n2_high, cots[0], cots_t[0], bias_b, gathered_b, None)
    out1, back1, up_bias1, dw1 = mlp(far_low, far_high, cots[1], cots_t[1], bias_b, gathered_b, dw0)
    up_bias_g = up_bias0 + up_bias1

    def sum_cores(parts):
        low = add_low(parts[0], tensor_swap(parts[1], 1))
        for bit in core_bits[1:]:
            low = add_low(low, tensor_swap(low, bit))
        return low

    back_far = tensor_swap(sum_cores(back1), pair_bit)
    back_low = add_low(sum_cores(back0), back_far)
    back_high = tensor_swap(back_low, 1)
    middle_grad, branch_grad, sums2 = by_rows(
        functools.partial(middle_back_kernel, width),
        [shaped((rows, half_pad), f32), shaped((rows, feats), bf16), shaped((4, half_pad), f32)],
        [False, False, True],
        [back_low, back_high, middle, cots[0], vectors],
        [False, False, False, False, True],
        rows,
        tile,
    )
    grad_b = scatter_units([scatter_rows(d, shard) for d in dw1], far_bits, add_low)

    def spread(blocks):
        got = [blocks[:share]]
        for i in range(1, groups):
            got.append(tensor_swap(blocks[i * share : (i + 1) * share], i * sub))
        for i in range(len(group_bits)):
            swapped = [got[n ^ (1 << i)] for n in range(groups)]
            got = [jnp.where((gi >> i) & 1 == 1, s, g) for s, g in zip(swapped, got)]
        return jnp.stack([g.T[:seq] for g in got])

    out_far = tensor_swap(sum_cores(out1), pair_bit)
    out_half = middle[:, :half_pad] + sum_cores(out0).astype(f32) + out_far.astype(f32)
    out_half = (out_half + vectors[5:6, :half_pad]).astype(bf16)
    layer_out = spread(nt(pick, out_half).astype(bf16))

    grad_o = scatter_rows(out_grad(branch_grad, [kept[u][2] for u in range(groups)]), shard)
    grad_o = [grad_o[:, u * heads * HD : (u + 1) * heads * HD] for u in range(groups)]
    grad_o = scatter_units(grad_o, far_bits + [pair_bit], add_low)
    back = None
    grads_a = [None] * groups
    biases_a = [None] * groups
    for u in range(groups)[::-1]:
        w, qkv_t, _, lse = kept[u]
        dw, biases_a[u], back = attend_back(xnt, branch_grad, w, qkv_t, lse, back, seq, heads)
        grads_a[u] = scatter_rows(dw, shard)
    grad_a = scatter_units(grads_a, far_bits + [pair_bit], add_low)
    back, back_other = other_cores(back)
    in_shares, sums1 = by_rows_turned(
        functools.partial(first_back_kernel, width), back, back_other, x, middle_grad, vectors, pick,
        rows, tile,
    )
    input_grad = spread(in_shares).astype(f32)

    vector_g = jnp.concatenate([sums2[:1], sums1, sums2[1:]])
    qv_g = jnp.concatenate(biases_a).reshape(groups, heads, 3, HD)[:, :, ::2].reshape(groups, qv)
    unit_g = jnp.concatenate([qv_g[: len(wires_b)], up_bias_g], axis=1)
    more_qv = qv_g[len(wires_b) :]
    sizes = vector_g.size
    got = tensor_swap(jnp.concatenate([vector_g.reshape(-1), more_qv.reshape(-1)]), pair_bit)
    vector_g = vector_g + got[:sizes].reshape(vector_g.shape)
    unit_g = unit_g + jnp.pad(got[sizes:].reshape(more_qv.shape), ((0, 0), (0, units)))
    for bit in far_bits[::-1]:
        keep = unit_g.shape[0] // 2
        got = tensor_swap(jnp.concatenate([vector_g.reshape(-1), unit_g[keep:].reshape(-1)]), bit)
        vector_g = vector_g + got[:sizes].reshape(vector_g.shape)
        unit_g = unit_g[:keep] + got[sizes:].reshape(unit_g[:keep].shape)
    held = split_blocks(vector_g, 1, 0, half)
    for bit in fsdp_bits(0):
        leave = [o for o in held if o & bit]
        sent = [held.pop(o).reshape(-1) for o in leave] + [unit_g.reshape(-1)]
        got = fsdp_swap(jnp.concatenate(sent), bit)
        for n, o in enumerate(leave):
            held[o ^ bit] = held[o ^ bit] + got[n * 6 * half : (n + 1) * 6 * half].reshape(6, half)
        unit_g = unit_g + got[len(leave) * 6 * half :].reshape(unit_g.shape)
    vector_g = swap_halves(jnp.concatenate([held[0], tensor_swap(held[0], 1)], axis=1), 1)
    grad_a = swap_halves(grad_a.astype(f32), 0)
    grad_o = swap_halves(grad_o.astype(f32), 0)
    grad_b = swap_halves(grad_b.astype(f32), 0)
    return (
        layer_out,
        input_grad,
        grad_a.reshape(shard, heads, 3 * HD),
        unit_g[0, :qv].reshape(heads, 2 * HD),
        grad_o.T.reshape(heads, HD, shard),
        vector_g[0],
        vector_g[1],
        vector_g[2],
        vector_g[3],
        vector_g[4],
        grad_b[:, :units],
        unit_g[0, qv:],
        grad_b[:, units:].T,
        vector_g[5],
    )


def by_rows_turned(kernel, own, other, x, grad, vectors, pick, rows, tile):
    feats = x.shape[1]
    half = grad.shape[1]
    wide = pick.shape[0]
    cut3 = pl.BlockSpec((2, tile, half), lambda i: (0, i, 0))
    whole = lambda shape: pl.BlockSpec(shape, lambda i: (0, 0))
    return pl.pallas_call(
        kernel,
        grid=(rows // tile,),
        in_specs=[
            cut3,
            cut3,
            pl.BlockSpec((tile, feats), lambda i: (i, 0)),
            pl.BlockSpec((tile, half), lambda i: (i, 0)),
            whole(vectors.shape),
            whole(pick.shape),
        ],
        out_specs=[pl.BlockSpec((wide, tile), lambda i: (0, i)), whole((2, half))],
        out_shape=[shaped((wide, rows), bf16), shaped((2, half), f32)],
        compiler_params=pltpu.CompilerParams(vmem_limit_bytes=40 * MIB),
        cost_estimate=pl.CostEstimate(
            flops=2 * rows * half * wide, bytes_accessed=rows * feats * 12, transcendentals=0
        ),
    )(own, other, x, grad, vectors, pick)


def solution(mesh):
    return jax.shard_map(
        body,
        mesh=mesh,
        in_specs=(
            P("fsdp", None, None),
            P("fsdp", None, None),
            P("fsdp", "tensor", None),
            P("tensor", None),
            P("tensor", None, "fsdp"),
            P("fsdp"),
            P("fsdp"),
            P("fsdp"),
            P("fsdp"),
            P("fsdp"),
            P("fsdp", "tensor"),
            P("tensor"),
            P("tensor", "fsdp"),
            P("fsdp"),
        ),
        out_specs=(
            P("fsdp", None, "tensor"),
            P("fsdp", None, "tensor"),
            P("fsdp", "tensor", None),
            P("tensor", None),
            P("tensor", None, "fsdp"),
            P("fsdp"),
            P("fsdp"),
            P("fsdp"),
            P("fsdp"),
            P("fsdp"),
            P("fsdp", "tensor"),
            P("tensor"),
            P("tensor", "fsdp"),
            P("fsdp"),
        ),
        check_vma=False,
    )
```

```python
import functools

import jax
import jax.numpy as jnp
from jax import lax
from jax.experimental import pallas as pl
from jax.experimental.pallas import tpu as pltpu
from jax.sharding import PartitionSpec as P

HD = 72
norm_eps = 1e-06
LOG2E = 1.4426950408889634
GELU_A = 0.7978845608028654
GELU_B = 0.044715
MIB = 1024 * 1024
bf16 = jnp.bfloat16
f32 = jnp.float32


def round_up(value, unit):
    return -(-value // unit) * unit


def nn(a, b):
    return lax.dot_general(a, b, (((1,), (0,)), ((), ())), preferred_element_type=f32)


def nt(a, b):
    return lax.dot_general(a, b, (((1,), (1,)), ((), ())), preferred_element_type=f32)


def shaped(shape, dtype):
    return jax.ShapeDtypeStruct(shape, dtype)


def on_chip(kernel, out_shape, args, scratch=(), flops=0, exps=0, after=()):
    whole = pl.BlockSpec(memory_space=pltpu.VMEM)
    count, extra = len(args), len(after)

    def run(*refs):
        kernel(*refs[:count], *refs[count + extra :])

    moved = sum(a.size * a.dtype.itemsize for a in list(args) + list(out_shape))
    return pl.pallas_call(
        run,
        in_specs=[whole] * count + [pl.BlockSpec(memory_space=pl.ANY)] * extra,
        out_specs=[whole] * len(out_shape),
        out_shape=list(out_shape),
        scratch_shapes=list(scratch),
        compiler_params=pltpu.CompilerParams(vmem_limit_bytes=60 * MIB),
        cost_estimate=pl.CostEstimate(flops=flops, bytes_accessed=moved, transcendentals=exps),
    )(*args, *after)


def fsdp_swap(x, bit):
    size = lax.axis_size("fsdp")
    return lax.ppermute(x, "fsdp", [(i, i ^ bit) for i in range(size)])


def tensor_swap(x, bit):
    size = lax.axis_size("tensor")
    return lax.ppermute(x, "tensor", [(i, i ^ bit) for i in range(size)])


def fsdp_bits(part):
    bits = []
    bit = 1
    while bit < lax.axis_size("fsdp"):
        bits.append(bit)
        bit *= 2
    return bits if part == 0 else bits[::-1]


def gather_pieces(own):
    half = own.shape[1] // 2
    arrays = [own]
    first = {}
    for bit in fsdp_bits(0):
        first[bit] = len(arrays)
        arrays.append(fsdp_swap(own, bit))
    plan = []
    for part in (0, 1):
        have = {0: (0, part * half)}
        for bit in fsdp_bits(part):
            new = {}
            for offset, (index, row) in have.items():
                if offset == 0:
                    new[bit] = (first[bit], part * half)
                else:
                    new[offset ^ bit] = (len(arrays), 0)
                    arrays.append(fsdp_swap(arrays[index][:, row : row + half], bit))
            have.update(new)
        plan.append([have[o] for o in range(len(have))])
    return arrays, plan


def assemble(out, refs, unit, plan, half, half_pad, start=0):
    for part in (0, 1):
        for offset, (index, row) in enumerate(plan[part]):
            at = part * half_pad + offset * half
            out[at : at + half, :] = refs[index][unit, row : row + half, start : start + out.shape[1]]
        used = len(plan[part]) * half
        if used < half_pad:
            out[part * half_pad + used : (part + 1) * half_pad, :] = jnp.zeros(
                (half_pad - used, out.shape[1]), out.dtype
            )


def add_low(a, b):
    return (a.astype(f32) + b.astype(f32)).astype(bf16)


def split_blocks(x, axis, start, size):
    return {
        n: lax.slice_in_dim(x, start + n * size, start + (n + 1) * size, axis=axis)
        for n in range(lax.axis_size("fsdp"))
    }


def payload_shapes(units, half, cols):
    held = lax.axis_size("fsdp") // 2 * half
    return [shaped((units, held, cols), bf16)] * 4


def emit(refs, unit, grad, half, at):
    count = lax.axis_size("fsdp")
    cols = grad.shape[1]
    for part in (0, 1):
        bit = fsdp_bits(part)[0]
        places = [0, 0]
        for offset in range(count):
            kept = 0 if offset & bit else 1
            row = part * (grad.shape[0] // 2) + offset * half
            to = places[kept] * half
            places[kept] += 1
            refs[2 * part + kept][unit, to : to + half, at : at + cols] = grad[row : row + half].astype(bf16)


def fold_kernel(stage, half, *refs):
    keeps, gots, outs = refs[:2], refs[2:4], refs[4:]
    for part in (0, 1):
        bits = fsdp_bits(part)
        offsets = [o for o in range(lax.axis_size("fsdp")) if not any(o & b for b in bits[: stage + 1])]
        places = [0, 0]
        for n, offset in enumerate(offsets):
            rows = slice(n * half, (n + 1) * half)
            total = add_low(keeps[part][:, rows, :], gots[part][:, rows, :])
            if stage + 1 == len(bits):
                outs[0][:, part * half : (part + 1) * half, :] = total
            else:
                kept = 0 if offset & bits[stage + 1] else 1
                to = places[kept] * half
                places[kept] += 1
                outs[2 * part + kept][:, to : to + half, :] = total


def send(payload, stage):
    return [fsdp_swap(payload[2 * part], fsdp_bits(part)[stage]) for part in (0, 1)]


def fold(payload, got, stage, after=()):
    keeps = [payload[1], payload[3]]
    units, held, cols = keeps[0].shape
    half = held // (lax.axis_size("fsdp") >> (stage + 1))
    if stage + 1 == len(fsdp_bits(0)):
        outs = [shaped((units, 2 * half, cols), bf16)]
    else:
        outs = [shaped((units, held // 2, cols), bf16)] * 4
    return on_chip(functools.partial(fold_kernel, stage, half), outs, keeps + got, after=after)


def finish(payload, after=()):
    stages = len(fsdp_bits(0))
    for stage in range(stages):
        payload = fold(payload, send(payload, stage), stage, after if stage == 0 else ())
    return payload[0]


def row_of(ref, unit, start, count, size):
    table = ref[unit, :, start : start + count].astype(f32).T
    return jnp.concatenate([table[n : n + 1] for n in range(count)], axis=1)[:, :size]


def attend_kernel(seq, heads, plan, count, chosen, first, *refs):
    xn_ref = refs[0]
    pieces = refs[1 : 1 + count]
    rest = refs[1 + count :]
    if not first:
        before_ref, rest = rest[0], rest[1:]
    part_ref = rest[4 * len(chosen)]
    rows, feats = xn_ref.shape
    half = feats // 2
    wide = heads * 3 * HD
    shard = pieces[0].shape[1]
    live = lax.broadcasted_iota(jnp.int32, (rows, 1), 0) < seq
    for place, unit in enumerate(chosen):
        w_ref, qkv_ref, ctx_ref, lse_ref = rest[4 * place : 4 * place + 4]
        assemble(w_ref, pieces, unit, plan, shard // 2, half)
        qv = row_of(pieces[0], unit, wide + heads * HD + 6, -(-heads * 2 * HD // shard), heads * 2 * HD)
        bias = []
        for h in range(heads):
            at = h * 2 * HD
            bias += [qv[:, at : at + HD], jnp.zeros((1, HD), f32), qv[:, at + HD : at + 2 * HD]]
        qkv = nn(xn_ref[...], w_ref[:, :wide]) + jnp.concatenate(bias, axis=1)
        qkv_t = qkv.T
        qkv_ref[...] = qkv_t.astype(bf16)
        contexts = []
        for h in range(heads):
            at = h * 3 * HD
            q_t = qkv_t[at : at + HD].astype(bf16)
            k_n = qkv[:, at + HD : at + 2 * HD].astype(bf16)
            v_t = qkv_t[at + 2 * HD : at + 3 * HD].astype(bf16)
            scores = nn(k_n, q_t) * (HD**-0.5 * LOG2E)
            scores = jnp.where(live, scores, -1e30)
            top = jnp.max(scores, axis=0, keepdims=True)
            weight = jnp.exp2(scores - top)
            total_weight = jnp.sum(weight, axis=0, keepdims=True)
            lse_ref[h : h + 1, :] = top + jnp.log2(total_weight)
            contexts.append(nn(v_t, weight.astype(bf16)) / total_weight)
        ctx = jnp.concatenate(contexts, axis=0).T.astype(bf16)
        ctx_ref[...] = ctx
        for n in (0, 1):
            add = nt(ctx, w_ref[n * half : (n + 1) * half, wide : wide + heads * HD])
            if place > 0:
                add = add + part_ref[n].astype(f32)
            elif not first:
                add = add + before_ref[n].astype(f32)
            part_ref[n] = add.astype(bf16)


def attend(xn, pieces, plan, chosen, before, seq, heads, after):
    rows, feats = xn.shape
    wide = heads * 3 * HD
    cols = wide + heads * HD
    units = len(chosen)
    args = [xn] + pieces + ([] if before is None else [before])
    found = on_chip(
        functools.partial(attend_kernel, seq, heads, plan, len(pieces), chosen, before is None),
        [
            shaped((feats, cols), bf16),
            shaped((wide, rows), bf16),
            shaped((rows, heads * HD), bf16),
            shaped((heads, rows), f32),
        ]
        * units
        + [shaped((2, rows, feats // 2), bf16)],
        args,
        flops=units * 2 * rows * (feats * cols + heads * 2 * rows * 256),
        exps=units * heads * rows * rows,
        after=after,
    )
    return [found[4 * u : 4 * u + 4] for u in range(units)], found[4 * units]


def attend_back_kernel(seq, heads, count, first, half, extra, *refs):
    xnt_ref, bg_ref = refs[:2]
    w_refs, qkv_refs, lse_refs = [refs[2 + n * count : 2 + (n + 1) * count] for n in range(3)]
    rest = refs[2 + 3 * count :]
    ctx_refs, rest = rest[: count * extra], rest[count * extra :]
    if not first:
        before_ref, rest = rest[0], rest[1:]
    payload, db_ref, part_ref = rest[:4], rest[4], rest[5]
    rows, feats = bg_ref.shape
    half_pad = feats // 2
    wide = heads * 3 * HD
    live = lax.broadcasted_iota(jnp.int32, (rows, 1), 0) < seq
    scale = HD**-0.5
    if extra:
        bg_t = bg_ref[...].astype(f32).T.astype(bf16)
        for unit in range(count):
            ctx = [r[...].astype(f32) for r in ctx_refs[unit * extra : (unit + 1) * extra]]
            emit(payload, unit, nn(bg_t, jnp.concatenate(ctx, axis=1).astype(bf16)), half, wide)
    for unit in range(count):
        w_ref = w_refs[unit]
        d_ctx_t = nn(bg_ref[...], w_ref[:, wide : wide + heads * HD]).T
        qkv_t = qkv_refs[unit][...].astype(f32)
        qkv = qkv_t.T
        pieces = []
        for h in range(heads):
            at = h * 3 * HD
            q_t = qkv_t[at : at + HD].astype(bf16)
            k_t = qkv_t[at + HD : at + 2 * HD].astype(bf16)
            k_n = qkv[:, at + HD : at + 2 * HD].astype(bf16)
            v_n = qkv[:, at + 2 * HD : at + 3 * HD].astype(bf16)
            d_o = d_ctx_t[h * HD : (h + 1) * HD].astype(bf16)
            scores = nn(k_n, q_t) * (scale * LOG2E)
            probs = jnp.where(live, jnp.exp2(scores - lse_refs[unit][h : h + 1, :]), 0.0)
            d_probs = nn(v_n, d_o)
            delta = jnp.sum(d_probs * probs, axis=0, keepdims=True)
            d_scores = (probs * (d_probs - delta)).astype(bf16)
            d_v = nt(probs.astype(bf16), d_o)
            d_k = nt(d_scores, q_t) * scale
            d_q = nn(k_t, d_scores) * scale
            pieces += [d_q.T, d_k, d_v]
        d_qkv = jnp.concatenate(pieces, axis=1).astype(bf16)
        db_ref[unit : unit + 1, :] = jnp.sum(d_qkv.astype(f32), axis=0, keepdims=True)
        emit(payload, unit, nn(xnt_ref[...], d_qkv), half, 0)
        for n in (0, 1):
            add = nt(d_qkv, w_ref[n * half_pad : (n + 1) * half_pad, :wide])
            if unit > 0:
                add = add + part_ref[n].astype(f32)
            elif not first:
                add = add + before_ref[n].astype(f32)
            part_ref[n] = add.astype(bf16)


def attend_back(xnt, bg, kept, contexts, before, seq, heads, half, after):
    rows, feats = bg.shape
    wide = heads * 3 * HD
    count = len(kept)
    extra = len(contexts) // count
    args = [xnt, bg] + [k[0] for k in kept] + [k[1] for k in kept] + [k[3] for k in kept] + contexts
    found = on_chip(
        functools.partial(attend_back_kernel, seq, heads, count, before is None, half, extra),
        payload_shapes(count, half, wide + extra * heads * HD)
        + [shaped((count, wide), f32), shaped((2, rows, feats // 2), bf16)],
        args + ([] if before is None else [before]),
        flops=count * 2 * rows * (2 * feats * wide + heads * 5 * rows * 256),
        exps=count * heads * rows * rows,
        after=after,
    )
    return found[:4], found[4], found[5]


def mlp_kernel(plan, counts, units, first, half, *refs):
    low_ref, high_ref, cot_ref, cott_ref = refs[:4]
    at = 4
    pieces = []
    for count in counts:
        pieces.append(refs[at : at + count])
        at += count
    if not first:
        before_refs, before_db = refs[at : at + len(counts)], refs[at + len(counts)]
        at += len(counts) + 1
    out_refs, back_refs, db_ref = refs[at : at + 2], refs[at + 2 : at + 4], refs[at + 4]
    at += 5
    dw_refs = refs[at : at + (len(counts) if first else 4)]
    n2_ref, n2t_ref, w_ref, out_sum, back_sum = refs[at + len(dw_refs) :]
    half_pad = low_ref.shape[1]
    n2_ref[:, :half_pad] = low_ref[...]
    n2_ref[:, half_pad:] = high_ref[...]
    n2t_ref[:half_pad, :] = low_ref[...].astype(f32).T.astype(bf16)
    n2t_ref[half_pad:, :] = high_ref[...].astype(f32).T.astype(bf16)
    for u in range(len(counts)):
        shard = pieces[u][0].shape[1]
        assemble(w_ref, pieces[u], 0, plan, shard // 2, half_pad)
        bias = row_of(pieces[u][0], 0, 2 * units, -(-units // shard), units)
        up = w_ref[:, :units]
        down = w_ref[:, units:]
        v = nn(n2_ref[...], up) + bias
        square = v * v
        t = jnp.tanh(GELU_A * v * (1.0 + GELU_B * square))
        hidden = (0.5 * v * (1.0 + t)).astype(bf16)
        slope = 0.5 * (1.0 + t) + (0.5 * GELU_A) * v * (1.0 - t * t) * (1.0 + 3.0 * GELU_B * square)
        pre_grad = (nn(cot_ref[...], down) * slope).astype(bf16)
        out_add = nt(hidden, down)
        back_add = nt(pre_grad, up)
        if u == 0:
            out_sum[...] = out_add
            back_sum[...] = back_add
        else:
            out_sum[...] += out_add
            back_sum[...] += back_add
        db = jnp.sum(pre_grad.astype(f32), axis=0, keepdims=True)
        db_ref[u : u + 1, :] = db if first else db + before_db[u : u + 1, :]
        d_up = nn(n2t_ref[...], pre_grad)
        d_down = nn(cott_ref[...], hidden)
        if first:
            dw_refs[u][:, :units] = d_up.astype(bf16)
            dw_refs[u][:, units:] = d_down.astype(bf16)
        else:
            emit(dw_refs, u, d_up + before_refs[u][:, :units].astype(f32), half, 0)
            emit(dw_refs, u, d_down + before_refs[u][:, units:].astype(f32), half, units)
    for n in (0, 1):
        out_refs[n][...] = out_sum[:, n * half_pad : (n + 1) * half_pad].astype(bf16)
        back_refs[n][...] = back_sum[:, n * half_pad : (n + 1) * half_pad].astype(bf16)


def mlp(low, high, cot, cot_t, gathered, units, before):
    rows, half_pad = low.shape
    feats = 2 * half_pad
    plan = gathered[0][1]
    half = gathered[0][0][0].shape[1] // 2
    count = len(gathered)
    args = [low, high, cot, cot_t] + [a for g in gathered for a in g[0]] + list(before or [])
    grads = [shaped((feats, 2 * units), bf16)] * count if before is None else payload_shapes(count, half, 2 * units)
    found = on_chip(
        functools.partial(mlp_kernel, plan, [len(g[0]) for g in gathered], units, before is None, half),
        [
            shaped((rows, half_pad), bf16),
            shaped((rows, half_pad), bf16),
            shaped((rows, half_pad), bf16),
            shaped((rows, half_pad), bf16),
            shaped((count, units), f32),
        ]
        + grads,
        args,
        scratch=[
            pltpu.VMEM((rows, feats), bf16),
            pltpu.VMEM((feats, rows), bf16),
            pltpu.VMEM((feats, 2 * units), bf16),
            pltpu.VMEM((rows, feats), f32),
            pltpu.VMEM((rows, feats), f32),
        ],
        flops=count * 12 * rows * feats * units,
        exps=count * rows * units,
    )
    return found[:2], found[2:4], found[4], found[5:]


def standardize(rows, width):
    mean = jnp.sum(rows, axis=-1, keepdims=True) / width
    var = jnp.sum(rows * rows, axis=-1, keepdims=True) / width - mean * mean
    rstd = lax.rsqrt(var + norm_eps)
    return (rows - mean) * rstd, rstd


def norm_back(grad, xhat, rstd, gain, width):
    a = grad * gain
    mean_a = jnp.sum(a, axis=-1, keepdims=True) / width
    mean_ax = jnp.sum(a * xhat, axis=-1, keepdims=True) / width
    return rstd * (a - mean_a - xhat * mean_ax)


def by_rows(kernel, out_shape, out_whole, args, whole, rows, tile, after=()):
    def spec(shape, uncut):
        if uncut:
            return pl.BlockSpec(shape, lambda i, n=len(shape): (0,) * n)
        if len(shape) == 3:
            return pl.BlockSpec((shape[0], tile, shape[2]), lambda i: (0, i, 0))
        return pl.BlockSpec((tile, shape[1]), lambda i: (i, 0))

    count, extra = len(args), len(after)

    def run(*refs):
        kernel(*refs[:count], *refs[count + extra :])

    return pl.pallas_call(
        run,
        grid=(rows // tile,),
        in_specs=[spec(a.shape, w) for a, w in zip(args, whole)]
        + [pl.BlockSpec(memory_space=pl.ANY)] * extra,
        out_specs=[spec(o.shape, w) for o, w in zip(out_shape, out_whole)],
        out_shape=list(out_shape),
        compiler_params=pltpu.CompilerParams(vmem_limit_bytes=40 * MIB),
        cost_estimate=pl.CostEstimate(
            flops=0,
            bytes_accessed=sum(a.size * a.dtype.itemsize for a in list(args) + list(out_shape)),
            transcendentals=0,
        ),
    )(*args, *after)


def joined(ref):
    return jnp.concatenate([ref[0].astype(f32), ref[1].astype(f32)], axis=-1)


def crossed(ref):
    return jnp.concatenate([ref[1].astype(f32), ref[0].astype(f32)], axis=-1)


def middle_kernel(width, x_ref, own_ref, other_ref, vec_ref, middle_ref, low_ref, high_ref):
    half = low_ref.shape[1]
    middle = x_ref[...].astype(f32) + joined(own_ref) + crossed(other_ref) + vec_ref[0:1, :]
    middle_ref[...] = middle
    xhat, rstd = standardize(middle, width)
    n2 = (xhat * vec_ref[3:4, :] + vec_ref[4:5, :]).astype(bf16)
    low_ref[...] = n2[:, :half]
    high_ref[...] = n2[:, half:]


def add_sums(ref, sums):
    @pl.when(pl.program_id(0) == 0)
    def _():
        ref[...] = sums

    @pl.when(pl.program_id(0) > 0)
    def _():
        ref[...] += sums


def column_sums(parts):
    return jnp.concatenate([jnp.sum(p, axis=0, keepdims=True) for p in parts], axis=0)


def middle_back_kernel(
    width, low_ref, high_ref, middle_ref, cot_ref, out_ref, more_ref, vec_ref,
    grad_ref, bg_ref, out_sum_ref, sum_ref,
):
    out_sum_ref[...] = add_low(out_ref[...], more_ref[...])
    half = low_ref.shape[1]
    grad = jnp.concatenate([low_ref[...].astype(f32), high_ref[...].astype(f32)], axis=-1)
    xhat, rstd = standardize(middle_ref[...], width)
    cot = cot_ref[...].astype(f32)
    back = cot + norm_back(grad, xhat, rstd, vec_ref[3:4, :], width)
    grad_ref[...] = back[:, :half]
    bg_ref[...] = back.astype(bf16)
    add_sums(
        sum_ref,
        column_sums([back[:, :half], grad[:, :half] * xhat[:, :half], grad[:, :half], cot[:, :half]]),
    )


def out_kernel(own_ref, other_ref, far_ref, middle_ref, _, vec_ref, pick_ref, out_ref):
    half = own_ref.shape[1]
    result = middle_ref[:, :half] + own_ref[...].astype(f32) + other_ref[...].astype(f32)
    result = result + far_ref[...].astype(f32) + vec_ref[5:6, :half]
    out_ref[...] = nt(pick_ref[...], result.astype(bf16)).astype(bf16)


def first_back_kernel(width, own_ref, other_ref, x_ref, grad_ref, _, vec_ref, pick_ref, out_ref, sum_ref):
    half = grad_ref.shape[1]
    grad = joined(own_ref) + crossed(other_ref)
    xhat, rstd = standardize(x_ref[...].astype(f32), width)
    back = norm_back(grad, xhat, rstd, vec_ref[1:2, :], width)
    result = (grad_ref[...] + back[:, :half]).astype(bf16)
    out_ref[...] = nt(pick_ref[...], result).astype(bf16)
    add_sums(sum_ref, column_sums([grad[:, :half] * xhat[:, :half], grad[:, :half]]))


def start_kernel(seq, turned, pick_ref, source_ref, *refs):
    count = (len(refs) - 1) // (2 + turned)
    ins, outs = refs[:count], refs[len(refs) - count * (1 + turned) :]
    width = ins[0].shape[2]
    place = lax.broadcasted_iota(jnp.int32, (width, source_ref.shape[1]), 0) == source_ref[...]
    place = jnp.where(place, 1.0, 0.0).astype(bf16)
    for n in range(count):
        outs[n][...] = jnp.zeros(outs[n].shape, bf16)
        outs[n][:seq, :] = nn(ins[n][0], place).astype(bf16)
        if turned:
            outs[count + n][...] = outs[n][...].astype(f32).T.astype(bf16)


def start(array, index, source, rows, turned, after):
    _, seq, width = array.shape
    feats = source.shape[0]
    count = index.shape[0]
    image = lambda n: pl.BlockSpec((1, seq, width), lambda i, pick: (pick[n], 0, 0))
    flat = lambda *shape: pl.BlockSpec(shape, lambda i, pick: (0, 0))
    return pl.pallas_call(
        functools.partial(start_kernel, seq, turned),
        grid_spec=pltpu.PrefetchScalarGridSpec(
            num_scalar_prefetch=1,
            grid=(1,),
            in_specs=[flat(1, feats)] + [image(n) for n in range(count)] + [pl.BlockSpec(memory_space=pl.ANY)],
            out_specs=[flat(rows, feats)] * count + [flat(feats, rows)] * (count * turned),
        ),
        out_shape=[shaped((rows, feats), bf16)] * count + [shaped((feats, rows), bf16)] * (count * turned),
        compiler_params=pltpu.CompilerParams(vmem_limit_bytes=60 * MIB),
        cost_estimate=pl.CostEstimate(
            flops=2 * count * rows * width * feats, bytes_accessed=6 * count * rows * feats, transcendentals=0
        ),
    )(index, source[None, :], *([array] * count), after)


def stack_kernel(*refs):
    for n, ref in enumerate(refs[:-1]):
        refs[-1][n] = ref[0]


def turn_kernel(vectors_ref, bias_ref, out_ref):
    spare = out_ref.shape[1] - vectors_ref.shape[0] - bias_ref.shape[0]
    rows = [vectors_ref[...].astype(f32), bias_ref[...].astype(f32)]
    if spare:
        rows.append(jnp.zeros((spare, out_ref.shape[0]), f32))
    out_ref[...] = jnp.concatenate(rows, axis=0).T.astype(bf16)


def pack_kernel(heads, calls, sums1_ref, sums2_ref, up_ref, *refs):
    out_ref = refs[-1]
    lanes = out_ref.shape[1]
    out_ref[...] = jnp.zeros(out_ref.shape, f32)
    out_ref[0:1, : sums2_ref.shape[1]] = sums2_ref[0:1, :]
    out_ref[1:3, : sums1_ref.shape[1]] = sums1_ref[...]
    out_ref[3:6, : sums2_ref.shape[1]] = sums2_ref[1:4, :]
    groups = sum(len(c) for c in calls)
    for call, ref in zip(calls, refs[:-1]):
        for n, unit in enumerate(call):
            for h in range(heads):
                at, to = h * 3 * HD, h * 2 * HD
                out_ref[6 + unit : 7 + unit, to : to + HD] = ref[n : n + 1, at : at + HD]
                out_ref[6 + unit : 7 + unit, to + HD : to + 2 * HD] = ref[n : n + 1, at + 2 * HD : at + 3 * HD]
    out_ref[6 + groups : 6 + groups + up_ref.shape[0], : up_ref.shape[1]] = up_ref[...]


def group_sum_kernel(groups, rows_q, rows_b, cut_b, own_ref, got_ref, out_ref):
    out_ref[...] = own_ref[...]
    out_ref[0:6, :] = own_ref[0:6, :] + got_ref[0:6, :]
    keep = rows_q // 2
    out_ref[6 : 6 + keep, :] = own_ref[6 : 6 + keep, :] + got_ref[6 + keep : 6 + rows_q, :]
    if cut_b:
        base, keep = 6 + groups, rows_b // 2
        out_ref[base : base + keep, :] = own_ref[base : base + keep, :] + got_ref[base + keep : base + rows_b, :]


def block_sum_kernel(bits, half, own_ref, got_ref, out_ref):
    out_ref[...] = own_ref[...] + got_ref[...]
    for offset in range(lax.axis_size("fsdp")):
        if not any(offset & b for b in bits):
            at, other = offset * half, (offset ^ bits[-1]) * half
            out_ref[0:6, at : at + half] = own_ref[0:6, at : at + half] + got_ref[0:6, other : other + half]


def add_kernel(*refs):
    total = refs[0][...].astype(f32)
    for ref in refs[1:-1]:
        total = total + ref[...].astype(f32)
    refs[-1][...] = total.astype(bf16)


def add_after(parts, after):
    return on_chip(add_kernel, [shaped(parts[0].shape, bf16)], parts, after=after)[0]


def first_kernel(width, plan, at, count, *refs):
    x_ref, pieces = refs[0], refs[1 : 1 + count]
    xn_ref, xnt_ref, vec_ref, table = refs[1 + count :]
    assemble(table, pieces, 0, plan, pieces[0].shape[1] // 2, x_ref.shape[1] // 2, at)
    vectors = table[...].astype(f32).T
    vec_ref[...] = vectors
    xhat, _ = standardize(x_ref[...].astype(f32), width)
    xn = xhat * vectors[1:2] + vectors[2:3]
    xn_ref[...] = xn.astype(bf16)
    xnt_ref[...] = xn.T.astype(bf16)


def first(x, pieces, plan, width, at, after):
    rows, feats = x.shape
    return on_chip(
        functools.partial(first_kernel, width, plan, at, len(pieces)),
        [shaped((rows, feats), bf16), shaped((feats, rows), bf16), shaped((8, feats), f32)],
        [x] + pieces,
        scratch=[pltpu.VMEM((feats, 8), bf16)],
        after=after,
    )


def body(
    inputs, cotangent, qkv_proj, qv_bias, out_proj, out_bias, gain_one, shift_one, gain_two,
    shift_two, up_proj, up_bias, down_proj, down_bias,
):
    fsdp, tensor = lax.axis_size("fsdp"), lax.axis_size("tensor")
    images, seq, width = inputs.shape
    groups = images
    sub = tensor // groups
    heads = qkv_proj.shape[1]
    units = up_proj.shape[1]
    shard = qkv_proj.shape[0]
    share = width // tensor
    half = shard // 2
    used = half * fsdp
    half_pad = round_up(used, 128)
    feats = 2 * half_pad
    rows = round_up(seq, 128)
    tile = rows // 3 if rows % 384 == 0 else 128
    wide = heads * 3 * HD
    qv = heads * 2 * HD
    fi, ti = lax.axis_index("fsdp"), lax.axis_index("tensor")
    gi, ci = ti // sub, ti % 2
    group_bits = []
    bit = 1
    while bit < groups:
        group_bits.append(bit * sub)
        bit *= 2
    pair_bit, far_bits = group_bits[0], group_bits[1:][::-1]
    core_bits = []
    bit = 1
    while bit < sub:
        core_bits.append(bit)
        bit *= 2

    def gather_units(x, bits):
        have = [x]
        for bit in bits:
            have = have + [tensor_swap(h, bit) for h in have]
        return have

    def scatter_units(have, bits, add):
        for bit in bits[::-1]:
            keep = len(have) // 2
            have = [add(a, tensor_swap(b, bit)) for a, b in zip(have[:keep], have[keep:])]
        return have[0]

    def swap_halves(x, axis):
        low = lax.slice_in_dim(x, 0, half, axis=axis)
        high = lax.slice_in_dim(x, half, 2 * half, axis=axis)
        a = jnp.where(ci == 0, low, high)
        b = jnp.where(ci == 0, high, low)
        return jnp.concatenate([a, b], axis=axis)

    def columns(vector):
        count = -(-vector.size // shard)
        return jnp.pad(vector, (0, count * shard - vector.size)).reshape(count, shard).T

    own_vectors = swap_halves(
        jnp.stack([out_bias, gain_one, shift_one, gain_two, shift_two, down_bias]), 1
    )
    qv_rows = -(-qv // shard)
    own_bias = jnp.pad(qv_bias.reshape(1, qv), ((0, 0), (0, qv_rows * shard - qv))).reshape(qv_rows, shard)
    own_columns = on_chip(
        turn_kernel, [shaped((shard, round_up(6 + qv_rows, 8)), bf16)], [own_vectors, own_bias]
    )[0]
    wire_a = jnp.concatenate(
        [qkv_proj.reshape(shard, wide), out_proj.reshape(heads * HD, shard).T], axis=1
    )
    wire_a = jnp.concatenate([swap_halves(wire_a, 0), own_columns], axis=1)
    wires_a = gather_units(wire_a[None], far_bits)
    wire_b = swap_halves(jnp.concatenate([up_proj, down_proj.T], axis=1), 0)
    wire_b = jnp.concatenate([wire_b, columns(up_bias)], axis=1)
    near = len(fsdp_bits(0)) + 1
    gathered_a = gather_pieces(wires_a[0])

    lane = jnp.arange(feats, dtype=jnp.int32)
    part, at = lane // half_pad, lane % half_pad
    block = jnp.minimum(at // half, fsdp - 1) ^ fi
    source = jnp.where(at < used, block * shard + (part ^ ci) * half + at % half, -1)
    wire_b = add_after([wire_b[None]], gathered_a[0][near:])
    x = start(inputs, gi[None], source, rows, 0, wire_b)[0]
    wires_a += [tensor_swap(wires_a[0], pair_bit)]
    wires_a += [tensor_swap(add_after([w], [x]), pair_bit) for w in wires_a[1:-1]]
    wires_b = gather_units(wire_b, far_bits)
    gathered_b = [gather_pieces(wires_b[0])]
    found = start(cotangent, jnp.stack([gi, gi ^ 1]), source, rows, 1, gathered_b[0][0][1])
    cots, cots_t = found[:2], found[2:]
    out_share = jnp.arange(groups * share, dtype=jnp.int32)
    out_first = ((gi ^ (out_share // share)) * sub + ti % sub) * share + out_share % share
    pick = (out_first[:, None] == source[None, :half_pad]).astype(bf16)

    xn, xnt, vectors = first(x, *gathered_a, width, wide + heads * HD, [])
    kept, attn = attend(xn, *gathered_a, (0,), None, seq, heads, [cots[0]])
    later = on_chip(
        stack_kernel, [shaped((groups - 1,) + wire_a.shape, bf16)], wires_a[1:], after=gathered_b[0][0][near:]
    )[0]
    later = gather_pieces(later)
    held = [add_after([w], later[0][1:near]) for w in wires_b[1:]]
    gathered_b += [gather_pieces(w) for w in held]
    more, attn = attend(xn, *later, tuple(range(groups - 2)), attn, seq, heads, held)
    kept += more
    early = [a for g in gathered_b[1:] for a in g[0][1:near]]
    more, attn = attend(xn, *later, (groups - 2,), attn, seq, heads, early)
    kept += more

    def other_cores(parts):
        other = tensor_swap(parts, 1)
        for bit in core_bits[1:]:
            more = tensor_swap(jnp.stack([parts, other]), bit)
            parts, other = add_low(parts, more[0]), add_low(other, more[1])
        return parts, other

    attn, attn_other = other_cores(attn)
    middle, n2_low, n2_high = by_rows(
        functools.partial(middle_kernel, width),
        [shaped((rows, feats), f32), shaped((rows, half_pad), bf16), shaped((rows, half_pad), bf16)],
        [False] * 3,
        [x, attn, attn_other, vectors],
        [False, False, False, True],
        rows,
        tile,
        after=[a for g in gathered_b[1:] for a in g[0][1:near]],
    )
    far_low = tensor_swap(n2_low, pair_bit)

    out0, back0, up_bias0, dw0 = mlp(n2_low, n2_high, cots[0], cots_t[0], gathered_b, units, None)
    far_low = add_after([far_low], [up_bias0])
    far_high = tensor_swap(far_low, 1)
    out1, back1, up_bias_g, payload_b = mlp(
        far_low, far_high, cots[1], cots_t[1], gathered_b, units, list(dw0) + [up_bias0]
    )
    got_b = send(payload_b, 0)

    def other_half(parts):
        other = tensor_swap(parts[1], 1)
        for bit in core_bits[1:]:
            other = add_low(other, tensor_swap(add_low(parts[0], other), bit))
        return other

    def sum_cores(parts):
        return add_after([parts[0], other_half(parts)], [])

    back_far = tensor_swap(sum_cores(back1), pair_bit)
    back_low = add_low(sum_cores(back0), back_far)
    back_high = tensor_swap(back_low, 1)
    middle_grad, branch_grad, out_sum, sums2 = by_rows(
        functools.partial(middle_back_kernel, width),
        [
            shaped((rows, half_pad), f32),
            shaped((rows, feats), bf16),
            shaped((rows, half_pad), bf16),
            shaped((4, half_pad), f32),
        ],
        [False, False, False, True],
        [back_low, back_high, middle, cots[0], out1[0], other_half(out1), vectors],
        [False] * 6 + [True],
        rows,
        tile,
    )
    def spread(blocks):
        got = [blocks[:share]]
        for i in range(1, groups):
            got.append(tensor_swap(blocks[i * share : (i + 1) * share], i * sub))
        return got

    def collect(got):
        for i in range(len(group_bits)):
            swapped = [got[n ^ (1 << i)] for n in range(groups)]
            got = [jnp.where((gi >> i) & 1 == 1, s, g) for s, g in zip(swapped, got)]
        return jnp.stack([g.T[:seq] for g in got])

    stages = len(fsdp_bits(0))

    def rest_of(waiting, after):
        for stage in range(1, stages):
            waiting = fold(waiting, send(waiting, stage), stage, after)
        return waiting[0]

    middle_unit = groups // 2
    calls = [list(range(middle_unit, groups))[::-1]] + [[u] for u in range(middle_unit)[::-1]]
    back = None
    bias_calls = []
    payloads = []
    out_far = tensor_swap(out_sum, pair_bit)
    waiting_b = fold(payload_b, got_b, 0, [branch_grad])
    needed = [waiting_b[0]]
    for n, call in enumerate(calls):
        contexts = [kept[v][2] for u in call for v in (u, u - middle_unit)] if n == 0 else []
        payload, bias_g, back = attend_back(
            xnt, branch_grad, [kept[u] for u in call], contexts, back, seq, heads, half, needed
        )
        payloads.append(payload)
        bias_calls.append(bias_g)
        needed = []
        if n == 0:
            out_shares = by_rows_turned(
                out_kernel, [out0[0], other_half(out0), out_far, middle, back, vectors, pick], rows, tile, []
            )[0]
            out_got = spread(out_shares)
            layer_out = collect(out_got)
            grad_b = rest_of(waiting_b, [back])
            needed = [grad_b]
        elif n == 1:
            waiting = fold(payloads[0], send(payloads[0], 0), 0, [back])
            needed = [waiting[0]]
    back_done = back
    back, back_other = other_cores(back)
    grad_b = scatter_units([grad_b[u] for u in range(len(wires_b))], far_bits, add_low)
    far = rest_of(waiting, [back_done] + out_got)
    near_sums = [fold(p, send(p, 0), 0, [back_done]) for p in payloads[1:-1]]
    in_shares, sums1 = by_rows_turned(
        functools.partial(first_back_kernel, width),
        [back, back_other, x, middle_grad, far, vectors, pick],
        rows,
        tile,
        [(2, half_pad)],
    )
    in_got = spread(in_shares)
    own = [rest_of(p, [in_shares])[0] for p in near_sums] + [finish(payloads[-1], in_got)[0]]
    own = own[::-1]
    both = wide + heads * HD
    got = tensor_swap(far[..., :both], pair_bit)
    grads_a = []
    for u in range(middle_unit):
        n = calls[0].index(u + middle_unit)
        grads_a.append(add_low(jnp.concatenate([own[u], far[n, :, both:]], axis=1), got[n]))
    grad_a = scatter_units(grads_a, far_bits, add_low)
    grad_a, grad_o = grad_a[:, :wide], grad_a[:, wide:]
    input_grad = collect(in_got).astype(f32)

    small = on_chip(
        functools.partial(pack_kernel, heads, calls),
        [shaped((16, round_up(max(half_pad, qv, units), 128)), f32)],
        [sums1, sums2, up_bias_g] + bias_calls,
    )[0]
    rows_q, rows_b = groups, len(wires_b)
    for bit in (far_bits + [pair_bit])[::-1]:
        cut_b = bit != pair_bit
        small = on_chip(
            functools.partial(group_sum_kernel, groups, rows_q, rows_b, cut_b),
            [shaped(small.shape, f32)],
            [small, tensor_swap(small, bit)],
        )[0]
        rows_q //= 2
        rows_b = rows_b // 2 if cut_b else rows_b
    done_bits = []
    for bit in fsdp_bits(0):
        done_bits.append(bit)
        small = on_chip(
            functools.partial(block_sum_kernel, tuple(done_bits), half),
            [shaped(small.shape, f32)],
            [small, fsdp_swap(small, bit)],
        )[0]
    own_vector_g = small[:6, :half]
    vector_g = swap_halves(jnp.concatenate([own_vector_g, tensor_swap(own_vector_g, 1)], axis=1), 1)
    qvbias_g = small[6, :qv].reshape(heads, 2 * HD)
    upbias_g = small[6 + groups, :units]
    grad_a = swap_halves(grad_a.astype(f32), 0)
    grad_o = swap_halves(grad_o.astype(f32), 0)
    grad_b = swap_halves(grad_b.astype(f32), 0)
    return (
        layer_out,
        input_grad,
        grad_a.reshape(shard, heads, 3 * HD),
        qvbias_g,
        grad_o.T.reshape(heads, HD, shard),
        vector_g[0],
        vector_g[1],
        vector_g[2],
        vector_g[3],
        vector_g[4],
        grad_b[:, :units],
        upbias_g,
        grad_b[:, units:].T,
        vector_g[5],
    )


def by_rows_turned(kernel, args, rows, tile, sums):
    wide = args[-1].shape[0]

    def spec(shape):
        if len(shape) == 3:
            return pl.BlockSpec((shape[0], tile, shape[2]), lambda i: (0, i, 0))
        return pl.BlockSpec((tile, shape[1]), lambda i: (i, 0))

    whole = lambda shape: pl.BlockSpec(shape, lambda i: (0, 0))
    return pl.pallas_call(
        kernel,
        grid=(rows // tile,),
        in_specs=[spec(a.shape) for a in args[:-3]]
        + [pl.BlockSpec(memory_space=pl.ANY)]
        + [whole(a.shape) for a in args[-2:]],
        out_specs=[pl.BlockSpec((wide, tile), lambda i: (0, i))] + [whole(shape) for shape in sums],
        out_shape=[shaped((wide, rows), bf16)] + [shaped(shape, f32) for shape in sums],
        compiler_params=pltpu.CompilerParams(vmem_limit_bytes=40 * MIB),
        cost_estimate=pl.CostEstimate(
            flops=2 * rows * args[-1].size, bytes_accessed=12 * rows * args[0].shape[-1], transcendentals=0
        ),
    )(*args)


def solution(mesh):
    return jax.shard_map(
        body,
        mesh=mesh,
        in_specs=(
            P("fsdp", None, None),
            P("fsdp", None, None),
            P("fsdp", "tensor", None),
            P("tensor", None),
            P("tensor", None, "fsdp"),
            P("fsdp"),
            P("fsdp"),
            P("fsdp"),
            P("fsdp"),
            P("fsdp"),
            P("fsdp", "tensor"),
            P("tensor"),
            P("tensor", "fsdp"),
            P("fsdp"),
        ),
        out_specs=(
            P("fsdp", None, "tensor"),
            P("fsdp", None, "tensor"),
            P("fsdp", "tensor", None),
            P("tensor", None),
            P("tensor", None, "fsdp"),
            P("fsdp"),
            P("fsdp"),
            P("fsdp"),
            P("fsdp"),
            P("fsdp"),
            P("fsdp", "tensor"),
            P("tensor"),
            P("tensor", "fsdp"),
            P("fsdp"),
        ),
        check_vma=False,
    )
```

```python
import functools

import jax
import jax.numpy as jnp
from jax import lax
from jax.experimental import pallas as pl
from jax.experimental.pallas import tpu as pltpu
from jax.sharding import PartitionSpec as P

HD = 72
norm_eps = 1e-06
LOG2E = 1.4426950408889634
GELU_A = 0.7978845608028654
GELU_B = 0.044715
MIB = 1024 * 1024
bf16 = jnp.bfloat16
f32 = jnp.float32


def round_up(value, unit):
    return -(-value // unit) * unit


def nn(a, b):
    return lax.dot_general(a, b, (((1,), (0,)), ((), ())), preferred_element_type=f32)


def nt(a, b):
    return lax.dot_general(a, b, (((1,), (1,)), ((), ())), preferred_element_type=f32)


def shaped(shape, dtype):
    return jax.ShapeDtypeStruct(shape, dtype)


def on_chip(kernel, out_shape, args, scratch=(), flops=0, exps=0, after=(), limit=12):
    whole = pl.BlockSpec(memory_space=pltpu.VMEM)
    count, extra = len(args), len(after)

    def run(*refs):
        kernel(*refs[:count], *refs[count + extra :])

    moved = sum(a.size * a.dtype.itemsize for a in list(args) + list(out_shape))
    return pl.pallas_call(
        run,
        in_specs=[whole] * count + [pl.BlockSpec(memory_space=pl.ANY)] * extra,
        out_specs=[whole] * len(out_shape),
        out_shape=list(out_shape),
        scratch_shapes=list(scratch),
        compiler_params=pltpu.CompilerParams(vmem_limit_bytes=limit * MIB),
        cost_estimate=pl.CostEstimate(flops=flops, bytes_accessed=moved, transcendentals=exps),
    )(*args, *after)


def fsdp_swap(x, bit):
    size = lax.axis_size("fsdp")
    return lax.ppermute(x, "fsdp", [(i, i ^ bit) for i in range(size)])


def tensor_swap(x, bit):
    size = lax.axis_size("tensor")
    return lax.ppermute(x, "tensor", [(i, i ^ bit) for i in range(size)])


def fsdp_bits(part):
    bits = []
    bit = 1
    while bit < lax.axis_size("fsdp"):
        bits.append(bit)
        bit *= 2
    return bits if part == 0 else bits[::-1]


def gather_pieces(own):
    half = own.shape[1] // 2
    arrays = [own]
    first = {}
    for bit in fsdp_bits(0):
        first[bit] = len(arrays)
        arrays.append(fsdp_swap(own, bit))
    plan = []
    for part in (0, 1):
        have = {0: (0, part * half)}
        for bit in fsdp_bits(part):
            new = {}
            for offset, (index, row) in have.items():
                if offset == 0:
                    new[bit] = (first[bit], part * half)
                else:
                    new[offset ^ bit] = (len(arrays), 0)
                    arrays.append(fsdp_swap(arrays[index][:, row : row + half], bit))
            have.update(new)
        plan.append([have[o] for o in range(len(have))])
    return arrays, plan


def assemble(out, refs, unit, plan, half, half_pad, start=0):
    for part in (0, 1):
        for offset, (index, row) in enumerate(plan[part]):
            at = part * half_pad + offset * half
            out[at : at + half, :] = refs[index][unit, row : row + half, start : start + out.shape[1]]
        used = len(plan[part]) * half
        if used < half_pad:
            out[part * half_pad + used : (part + 1) * half_pad, :] = jnp.zeros(
                (half_pad - used, out.shape[1]), out.dtype
            )


def add_low(a, b):
    return (a.astype(f32) + b.astype(f32)).astype(bf16)


def split_blocks(x, axis, start, size):
    return {
        n: lax.slice_in_dim(x, start + n * size, start + (n + 1) * size, axis=axis)
        for n in range(lax.axis_size("fsdp"))
    }


def payload_shapes(units, half, cols):
    held = lax.axis_size("fsdp") // 2 * half
    return [shaped((units, held, cols), bf16)] * 4


def emit(refs, unit, grad, half, at):
    count = lax.axis_size("fsdp")
    cols = grad.shape[1]
    for part in (0, 1):
        bit = fsdp_bits(part)[0]
        places = [0, 0]
        for offset in range(count):
            kept = 0 if offset & bit else 1
            row = part * (grad.shape[0] // 2) + offset * half
            to = places[kept] * half
            places[kept] += 1
            refs[2 * part + kept][unit, to : to + half, at : at + cols] = grad[row : row + half].astype(bf16)


def fold_kernel(stage, half, *refs):
    keeps, gots, outs = refs[:2], refs[2:4], refs[4:]
    for part in (0, 1):
        bits = fsdp_bits(part)
        offsets = [o for o in range(lax.axis_size("fsdp")) if not any(o & b for b in bits[: stage + 1])]
        places = [0, 0]
        for n, offset in enumerate(offsets):
            rows = slice(n * half, (n + 1) * half)
            total = add_low(keeps[part][:, rows, :], gots[part][:, rows, :])
            if stage + 1 == len(bits):
                outs[0][:, part * half : (part + 1) * half, :] = total
            else:
                kept = 0 if offset & bits[stage + 1] else 1
                to = places[kept] * half
                places[kept] += 1
                outs[2 * part + kept][:, to : to + half, :] = total


def send(payload, stage):
    return [fsdp_swap(payload[2 * part], fsdp_bits(part)[stage]) for part in (0, 1)]


def fold(payload, got, stage, after=()):
    keeps = [payload[1], payload[3]]
    units, held, cols = keeps[0].shape
    half = held // (lax.axis_size("fsdp") >> (stage + 1))
    if stage + 1 == len(fsdp_bits(0)):
        outs = [shaped((units, 2 * half, cols), bf16)]
    else:
        outs = [shaped((units, held // 2, cols), bf16)] * 4
    return on_chip(functools.partial(fold_kernel, stage, half), outs, keeps + got, after=after)


def finish(payload, after=()):
    stages = len(fsdp_bits(0))
    for stage in range(stages):
        payload = fold(payload, send(payload, stage), stage, after if stage == 0 else ())
    return payload[0]


def row_of(ref, unit, start, count, size):
    table = ref[unit, :, start : start + count].astype(f32).T
    return jnp.concatenate([table[n : n + 1] for n in range(count)], axis=1)[:, :size]


def attend_kernel(seq, heads, plan, count, chosen, first, *refs):
    xn_ref = refs[0]
    pieces = refs[1 : 1 + count]
    rest = refs[1 + count :]
    if not first:
        before_ref, rest = rest[0], rest[1:]
    part_ref = rest[4 * len(chosen)]
    rows, feats = xn_ref.shape
    half = feats // 2
    wide = heads * 3 * HD
    shard = pieces[0].shape[1]
    live = lax.broadcasted_iota(jnp.int32, (rows, 1), 0) < seq
    for place, unit in enumerate(chosen):
        w_ref, qkv_ref, ctx_ref, lse_ref = rest[4 * place : 4 * place + 4]
        assemble(w_ref, pieces, unit, plan, shard // 2, half)
        qv = row_of(pieces[0], unit, wide + heads * HD + 6, -(-heads * 2 * HD // shard), heads * 2 * HD)
        bias = []
        for h in range(heads):
            at = h * 2 * HD
            bias += [qv[:, at : at + HD], jnp.zeros((1, HD), f32), qv[:, at + HD : at + 2 * HD]]
        qkv = nn(xn_ref[...], w_ref[:, :wide]) + jnp.concatenate(bias, axis=1)
        qkv_t = qkv.T
        qkv_ref[...] = qkv_t.astype(bf16)
        contexts = []
        for h in range(heads):
            at = h * 3 * HD
            q_t = qkv_t[at : at + HD].astype(bf16)
            k_n = qkv[:, at + HD : at + 2 * HD].astype(bf16)
            v_t = qkv_t[at + 2 * HD : at + 3 * HD].astype(bf16)
            scores = nn(k_n, q_t) * (HD**-0.5 * LOG2E)
            scores = jnp.where(live, scores, -1e30)
            top = jnp.max(scores, axis=0, keepdims=True)
            weight = jnp.exp2(scores - top)
            total_weight = jnp.sum(weight, axis=0, keepdims=True)
            lse_ref[h : h + 1, :] = top + jnp.log2(total_weight)
            contexts.append(nn(v_t, weight.astype(bf16)) / total_weight)
        ctx = jnp.concatenate(contexts, axis=0).T.astype(bf16)
        ctx_ref[...] = ctx
        for n in (0, 1):
            add = nt(ctx, w_ref[n * half : (n + 1) * half, wide : wide + heads * HD])
            if place > 0:
                add = add + part_ref[n].astype(f32)
            elif not first:
                add = add + before_ref[n].astype(f32)
            part_ref[n] = add.astype(bf16)


def attend(xn, pieces, plan, chosen, before, seq, heads, after):
    rows, feats = xn.shape
    wide = heads * 3 * HD
    cols = wide + heads * HD
    units = len(chosen)
    args = [xn] + pieces + ([] if before is None else [before])
    found = on_chip(
        functools.partial(attend_kernel, seq, heads, plan, len(pieces), chosen, before is None),
        [
            shaped((feats, cols), bf16),
            shaped((wide, rows), bf16),
            shaped((rows, heads * HD), bf16),
            shaped((heads, rows), f32),
        ]
        * units
        + [shaped((2, rows, feats // 2), bf16)],
        args,
        flops=units * 2 * rows * (feats * cols + heads * 2 * rows * 256),
        exps=units * heads * rows * rows,
        after=after,
        limit=20,
    )
    return [found[4 * u : 4 * u + 4] for u in range(units)], found[4 * units]


def attend_back_kernel(seq, heads, count, first, half, extra, *refs):
    xnt_ref, bg_ref = refs[:2]
    w_refs, qkv_refs, lse_refs = [refs[2 + n * count : 2 + (n + 1) * count] for n in range(3)]
    rest = refs[2 + 3 * count :]
    ctx_refs, rest = rest[: count * extra], rest[count * extra :]
    if not first:
        before_ref, rest = rest[0], rest[1:]
    payload, db_ref, part_ref = rest[:4], rest[4], rest[5]
    rows, feats = bg_ref.shape
    half_pad = feats // 2
    wide = heads * 3 * HD
    live = lax.broadcasted_iota(jnp.int32, (rows, 1), 0) < seq
    scale = HD**-0.5
    if extra:
        bg_t = bg_ref[...].astype(f32).T.astype(bf16)
        for unit in range(count):
            ctx = [r[...].astype(f32) for r in ctx_refs[unit * extra : (unit + 1) * extra]]
            emit(payload, unit, nn(bg_t, jnp.concatenate(ctx, axis=1).astype(bf16)), half, wide)
    for unit in range(count):
        w_ref = w_refs[unit]
        d_ctx_t = nn(bg_ref[...], w_ref[:, wide : wide + heads * HD]).T
        qkv_t = qkv_refs[unit][...].astype(f32)
        qkv = qkv_t.T
        pieces = []
        for h in range(heads):
            at = h * 3 * HD
            q_t = qkv_t[at : at + HD].astype(bf16)
            k_t = qkv_t[at + HD : at + 2 * HD].astype(bf16)
            k_n = qkv[:, at + HD : at + 2 * HD].astype(bf16)
            v_n = qkv[:, at + 2 * HD : at + 3 * HD].astype(bf16)
            d_o = d_ctx_t[h * HD : (h + 1) * HD].astype(bf16)
            scores = nn(k_n, q_t) * (scale * LOG2E)
            probs = jnp.where(live, jnp.exp2(scores - lse_refs[unit][h : h + 1, :]), 0.0)
            d_probs = nn(v_n, d_o)
            delta = jnp.sum(d_probs * probs, axis=0, keepdims=True)
            d_scores = (probs * (d_probs - delta)).astype(bf16)
            d_v = nt(probs.astype(bf16), d_o)
            d_k = nt(d_scores, q_t) * scale
            d_q = nn(k_t, d_scores) * scale
            pieces += [d_q.T, d_k, d_v]
        d_qkv = jnp.concatenate(pieces, axis=1).astype(bf16)
        db_ref[unit : unit + 1, :] = jnp.sum(d_qkv.astype(f32), axis=0, keepdims=True)
        emit(payload, unit, nn(xnt_ref[...], d_qkv), half, 0)
        for n in (0, 1):
            add = nt(d_qkv, w_ref[n * half_pad : (n + 1) * half_pad, :wide])
            if unit > 0:
                add = add + part_ref[n].astype(f32)
            elif not first:
                add = add + before_ref[n].astype(f32)
            part_ref[n] = add.astype(bf16)


def attend_back(xnt, bg, kept, contexts, before, seq, heads, half, after):
    rows, feats = bg.shape
    wide = heads * 3 * HD
    count = len(kept)
    extra = len(contexts) // count
    args = [xnt, bg] + [k[0] for k in kept] + [k[1] for k in kept] + [k[3] for k in kept] + contexts
    found = on_chip(
        functools.partial(attend_back_kernel, seq, heads, count, before is None, half, extra),
        payload_shapes(count, half, wide + extra * heads * HD)
        + [shaped((count, wide), f32), shaped((2, rows, feats // 2), bf16)],
        args + ([] if before is None else [before]),
        flops=count * 2 * rows * (2 * feats * wide + heads * 5 * rows * 256),
        exps=count * heads * rows * rows,
        after=after,
        limit=32,
    )
    return found[:4], found[4], found[5]


def mlp_kernel(plan, counts, units, first, half, *refs):
    low_ref, high_ref, cot_ref, cott_ref = refs[:4]
    at = 4
    pieces = []
    for count in counts:
        pieces.append(refs[at : at + count])
        at += count
    if not first:
        before_refs, before_db = refs[at : at + len(counts)], refs[at + len(counts)]
        at += len(counts) + 1
    out_refs, back_refs, db_ref = refs[at : at + 2], refs[at + 2 : at + 4], refs[at + 4]
    at += 5
    dw_refs = refs[at : at + (len(counts) if first else 4)]
    n2_ref, n2t_ref, w_ref, out_sum, back_sum = refs[at + len(dw_refs) :]
    half_pad = low_ref.shape[1]
    n2_ref[:, :half_pad] = low_ref[...]
    n2_ref[:, half_pad:] = high_ref[...]
    n2t_ref[:half_pad, :] = low_ref[...].astype(f32).T.astype(bf16)
    n2t_ref[half_pad:, :] = high_ref[...].astype(f32).T.astype(bf16)
    for u in range(len(counts)):
        shard = pieces[u][0].shape[1]
        assemble(w_ref, pieces[u], 0, plan, shard // 2, half_pad)
        bias = row_of(pieces[u][0], 0, 2 * units, -(-units // shard), units)
        up = w_ref[:, :units]
        down = w_ref[:, units:]
        v = nn(n2_ref[...], up) + bias
        square = v * v
        t = jnp.tanh(GELU_A * v * (1.0 + GELU_B * square))
        hidden = (0.5 * v * (1.0 + t)).astype(bf16)
        slope = 0.5 * (1.0 + t) + (0.5 * GELU_A) * v * (1.0 - t * t) * (1.0 + 3.0 * GELU_B * square)
        pre_grad = (nn(cot_ref[...], down) * slope).astype(bf16)
        out_add = nt(hidden, down)
        back_add = nt(pre_grad, up)
        if u == 0:
            out_sum[...] = out_add
            back_sum[...] = back_add
        else:
            out_sum[...] += out_add
            back_sum[...] += back_add
        db = jnp.sum(pre_grad.astype(f32), axis=0, keepdims=True)
        db_ref[u : u + 1, :] = db if first else db + before_db[u : u + 1, :]
        d_up = nn(n2t_ref[...], pre_grad)
        d_down = nn(cott_ref[...], hidden)
        if first:
            dw_refs[u][:, :units] = d_up.astype(bf16)
            dw_refs[u][:, units:] = d_down.astype(bf16)
        else:
            emit(dw_refs, u, d_up + before_refs[u][:, :units].astype(f32), half, 0)
            emit(dw_refs, u, d_down + before_refs[u][:, units:].astype(f32), half, units)
    for n in (0, 1):
        out_refs[n][...] = out_sum[:, n * half_pad : (n + 1) * half_pad].astype(bf16)
        back_refs[n][...] = back_sum[:, n * half_pad : (n + 1) * half_pad].astype(bf16)


def mlp(low, high, cot, cot_t, gathered, units, before):
    rows, half_pad = low.shape
    feats = 2 * half_pad
    plan = gathered[0][1]
    half = gathered[0][0][0].shape[1] // 2
    count = len(gathered)
    args = [low, high, cot, cot_t] + [a for g in gathered for a in g[0]] + list(before or [])
    grads = [shaped((feats, 2 * units), bf16)] * count if before is None else payload_shapes(count, half, 2 * units)
    found = on_chip(
        functools.partial(mlp_kernel, plan, [len(g[0]) for g in gathered], units, before is None, half),
        [
            shaped((rows, half_pad), bf16),
            shaped((rows, half_pad), bf16),
            shaped((rows, half_pad), bf16),
            shaped((rows, half_pad), bf16),
            shaped((count, units), f32),
        ]
        + grads,
        args,
        scratch=[
            pltpu.VMEM((rows, feats), bf16),
            pltpu.VMEM((feats, rows), bf16),
            pltpu.VMEM((feats, 2 * units), bf16),
            pltpu.VMEM((rows, feats), f32),
            pltpu.VMEM((rows, feats), f32),
        ],
        flops=count * 12 * rows * feats * units,
        exps=count * rows * units,
        limit=46,
    )
    return found[:2], found[2:4], found[4], found[5:]


def standardize(rows, width):
    mean = jnp.sum(rows, axis=-1, keepdims=True) / width
    var = jnp.sum(rows * rows, axis=-1, keepdims=True) / width - mean * mean
    rstd = lax.rsqrt(var + norm_eps)
    return (rows - mean) * rstd, rstd


def norm_back(grad, xhat, rstd, gain, width):
    a = grad * gain
    mean_a = jnp.sum(a, axis=-1, keepdims=True) / width
    mean_ax = jnp.sum(a * xhat, axis=-1, keepdims=True) / width
    return rstd * (a - mean_a - xhat * mean_ax)


def by_rows(kernel, out_shape, out_whole, args, whole, rows, tile, after=()):
    def spec(shape, uncut):
        if uncut:
            return pl.BlockSpec(shape, lambda i, n=len(shape): (0,) * n)
        if len(shape) == 3:
            return pl.BlockSpec((shape[0], tile, shape[2]), lambda i: (0, i, 0))
        return pl.BlockSpec((tile, shape[1]), lambda i: (i, 0))

    count, extra = len(args), len(after)

    def run(*refs):
        kernel(*refs[:count], *refs[count + extra :])

    return pl.pallas_call(
        run,
        grid=(rows // tile,),
        in_specs=[spec(a.shape, w) for a, w in zip(args, whole)]
        + [pl.BlockSpec(memory_space=pl.ANY)] * extra,
        out_specs=[spec(o.shape, w) for o, w in zip(out_shape, out_whole)],
        out_shape=list(out_shape),
        compiler_params=pltpu.CompilerParams(vmem_limit_bytes=16 * MIB),
        cost_estimate=pl.CostEstimate(
            flops=0,
            bytes_accessed=sum(a.size * a.dtype.itemsize for a in list(args) + list(out_shape)),
            transcendentals=0,
        ),
    )(*args, *after)


def joined(ref):
    return jnp.concatenate([ref[0].astype(f32), ref[1].astype(f32)], axis=-1)


def crossed(ref):
    return jnp.concatenate([ref[1].astype(f32), ref[0].astype(f32)], axis=-1)


def middle_kernel(width, x_ref, own_ref, other_ref, vec_ref, middle_ref, low_ref, high_ref):
    half = low_ref.shape[1]
    middle = x_ref[...].astype(f32) + joined(own_ref) + crossed(other_ref) + vec_ref[0:1, :]
    middle_ref[...] = middle
    xhat, rstd = standardize(middle, width)
    n2 = (xhat * vec_ref[3:4, :] + vec_ref[4:5, :]).astype(bf16)
    low_ref[...] = n2[:, :half]
    high_ref[...] = n2[:, half:]


def add_sums(ref, sums):
    @pl.when(pl.program_id(0) == 0)
    def _():
        ref[...] = sums

    @pl.when(pl.program_id(0) > 0)
    def _():
        ref[...] += sums


def column_sums(parts):
    return jnp.concatenate([jnp.sum(p, axis=0, keepdims=True) for p in parts], axis=0)


def middle_back_kernel(
    width, low_ref, high_ref, middle_ref, cot_ref, out_ref, more_ref, vec_ref,
    grad_ref, bg_ref, out_sum_ref, sum_ref,
):
    out_sum_ref[...] = add_low(out_ref[...], more_ref[...])
    half = low_ref.shape[1]
    grad = jnp.concatenate([low_ref[...].astype(f32), high_ref[...].astype(f32)], axis=-1)
    xhat, rstd = standardize(middle_ref[...], width)
    cot = cot_ref[...].astype(f32)
    back = cot + norm_back(grad, xhat, rstd, vec_ref[3:4, :], width)
    grad_ref[...] = back[:, :half]
    bg_ref[...] = back.astype(bf16)
    add_sums(
        sum_ref,
        column_sums([back[:, :half], grad[:, :half] * xhat[:, :half], grad[:, :half], cot[:, :half]]),
    )


def out_kernel(own_ref, other_ref, far_ref, middle_ref, _, vec_ref, pick_ref, out_ref):
    half = own_ref.shape[1]
    result = middle_ref[:, :half] + own_ref[...].astype(f32) + other_ref[...].astype(f32)
    result = result + far_ref[...].astype(f32) + vec_ref[5:6, :half]
    out_ref[...] = nt(pick_ref[...], result.astype(bf16)).astype(bf16)


def first_back_kernel(width, own_ref, other_ref, x_ref, grad_ref, _, vec_ref, pick_ref, out_ref, sum_ref):
    half = grad_ref.shape[1]
    grad = joined(own_ref) + crossed(other_ref)
    xhat, rstd = standardize(x_ref[...].astype(f32), width)
    back = norm_back(grad, xhat, rstd, vec_ref[1:2, :], width)
    result = (grad_ref[...] + back[:, :half]).astype(bf16)
    out_ref[...] = nt(pick_ref[...], result).astype(bf16)
    add_sums(sum_ref, column_sums([grad[:, :half] * xhat[:, :half], grad[:, :half]]))


def start_kernel(seq, turned, pick_ref, source_ref, *refs):
    count = (len(refs) - 1) // (2 + turned)
    ins, outs = refs[:count], refs[len(refs) - count * (1 + turned) :]
    width = ins[0].shape[2]
    place = lax.broadcasted_iota(jnp.int32, (width, source_ref.shape[1]), 0) == source_ref[...]
    place = jnp.where(place, 1.0, 0.0).astype(bf16)
    for n in range(count):
        outs[n][...] = jnp.zeros(outs[n].shape, bf16)
        outs[n][:seq, :] = nn(ins[n][0], place).astype(bf16)
        if turned:
            outs[count + n][...] = outs[n][...].astype(f32).T.astype(bf16)


def start(array, index, source, rows, turned, after):
    _, seq, width = array.shape
    feats = source.shape[0]
    count = index.shape[0]
    image = lambda n: pl.BlockSpec((1, seq, width), lambda i, pick: (pick[n], 0, 0))
    flat = lambda *shape: pl.BlockSpec(shape, lambda i, pick: (0, 0))
    return pl.pallas_call(
        functools.partial(start_kernel, seq, turned),
        grid_spec=pltpu.PrefetchScalarGridSpec(
            num_scalar_prefetch=1,
            grid=(1,),
            in_specs=[flat(1, feats)] + [image(n) for n in range(count)] + [pl.BlockSpec(memory_space=pl.ANY)],
            out_specs=[flat(rows, feats)] * count + [flat(feats, rows)] * (count * turned),
        ),
        out_shape=[shaped((rows, feats), bf16)] * count + [shaped((feats, rows), bf16)] * (count * turned),
        compiler_params=pltpu.CompilerParams(vmem_limit_bytes=(32 if turned else 20) * MIB),
        cost_estimate=pl.CostEstimate(
            flops=2 * count * rows * width * feats, bytes_accessed=6 * count * rows * feats, transcendentals=0
        ),
    )(index, source[None, :], *([array] * count), after)


def stack_kernel(*refs):
    for n, ref in enumerate(refs[:-1]):
        refs[-1][n] = ref[0]


def turn_kernel(vectors_ref, bias_ref, out_ref):
    spare = out_ref.shape[1] - vectors_ref.shape[0] - bias_ref.shape[0]
    rows = [vectors_ref[...].astype(f32), bias_ref[...].astype(f32)]
    if spare:
        rows.append(jnp.zeros((spare, out_ref.shape[0]), f32))
    out_ref[...] = jnp.concatenate(rows, axis=0).T.astype(bf16)


def pack_kernel(heads, calls, sums1_ref, sums2_ref, up_ref, *refs):
    out_ref = refs[-1]
    lanes = out_ref.shape[1]
    out_ref[...] = jnp.zeros(out_ref.shape, f32)
    out_ref[0:1, : sums2_ref.shape[1]] = sums2_ref[0:1, :]
    out_ref[1:3, : sums1_ref.shape[1]] = sums1_ref[...]
    out_ref[3:6, : sums2_ref.shape[1]] = sums2_ref[1:4, :]
    groups = sum(len(c) for c in calls)
    for call, ref in zip(calls, refs[:-1]):
        for n, unit in enumerate(call):
            for h in range(heads):
                at, to = h * 3 * HD, h * 2 * HD
                out_ref[6 + unit : 7 + unit, to : to + HD] = ref[n : n + 1, at : at + HD]
                out_ref[6 + unit : 7 + unit, to + HD : to + 2 * HD] = ref[n : n + 1, at + 2 * HD : at + 3 * HD]
    out_ref[6 + groups : 6 + groups + up_ref.shape[0], : up_ref.shape[1]] = up_ref[...]


def group_sum_kernel(groups, rows_q, rows_b, cut_b, own_ref, got_ref, out_ref):
    out_ref[...] = own_ref[...]
    out_ref[0:6, :] = own_ref[0:6, :] + got_ref[0:6, :]
    keep = rows_q // 2
    out_ref[6 : 6 + keep, :] = own_ref[6 : 6 + keep, :] + got_ref[6 + keep : 6 + rows_q, :]
    if cut_b:
        base, keep = 6 + groups, rows_b // 2
        out_ref[base : base + keep, :] = own_ref[base : base + keep, :] + got_ref[base + keep : base + rows_b, :]


def block_sum_kernel(bits, half, own_ref, got_ref, out_ref):
    out_ref[...] = own_ref[...] + got_ref[...]
    for offset in range(lax.axis_size("fsdp")):
        if not any(offset & b for b in bits):
            at, other = offset * half, (offset ^ bits[-1]) * half
            out_ref[0:6, at : at + half] = own_ref[0:6, at : at + half] + got_ref[0:6, other : other + half]


def add_kernel(*refs):
    total = refs[0][...].astype(f32)
    for ref in refs[1:-1]:
        total = total + ref[...].astype(f32)
    refs[-1][...] = total.astype(bf16)


def add_after(parts, after):
    return on_chip(add_kernel, [shaped(parts[0].shape, bf16)], parts, after=after)[0]


def first_kernel(width, plan, at, count, *refs):
    x_ref, pieces = refs[0], refs[1 : 1 + count]
    xn_ref, xnt_ref, vec_ref, table = refs[1 + count :]
    assemble(table, pieces, 0, plan, pieces[0].shape[1] // 2, x_ref.shape[1] // 2, at)
    vectors = table[...].astype(f32).T
    vec_ref[...] = vectors
    xhat, _ = standardize(x_ref[...].astype(f32), width)
    xn = xhat * vectors[1:2] + vectors[2:3]
    xn_ref[...] = xn.astype(bf16)
    xnt_ref[...] = xn.T.astype(bf16)


def first(x, pieces, plan, width, at, after):
    rows, feats = x.shape
    return on_chip(
        functools.partial(first_kernel, width, plan, at, len(pieces)),
        [shaped((rows, feats), bf16), shaped((feats, rows), bf16), shaped((8, feats), f32)],
        [x] + pieces,
        scratch=[pltpu.VMEM((feats, 8), bf16)],
        after=after,
        limit=16,
    )


def body(
    inputs, cotangent, qkv_proj, qv_bias, out_proj, out_bias, gain_one, shift_one, gain_two,
    shift_two, up_proj, up_bias, down_proj, down_bias,
):
    fsdp, tensor = lax.axis_size("fsdp"), lax.axis_size("tensor")
    images, seq, width = inputs.shape
    groups = images
    sub = tensor // groups
    heads = qkv_proj.shape[1]
    units = up_proj.shape[1]
    shard = qkv_proj.shape[0]
    share = width // tensor
    half = shard // 2
    used = half * fsdp
    half_pad = round_up(used, 128)
    feats = 2 * half_pad
    rows = round_up(seq, 128)
    tile = rows // 3 if rows % 384 == 0 else 128
    wide = heads * 3 * HD
    qv = heads * 2 * HD
    fi, ti = lax.axis_index("fsdp"), lax.axis_index("tensor")
    gi, ci = ti // sub, ti % 2
    group_bits = []
    bit = 1
    while bit < groups:
        group_bits.append(bit * sub)
        bit *= 2
    pair_bit, far_bits = group_bits[0], group_bits[1:][::-1]
    core_bits = []
    bit = 1
    while bit < sub:
        core_bits.append(bit)
        bit *= 2

    def gather_units(x, bits):
        have = [x]
        for bit in bits:
            have = have + [tensor_swap(h, bit) for h in have]
        return have

    def scatter_units(have, bits, add):
        for bit in bits[::-1]:
            keep = len(have) // 2
            have = [add(a, tensor_swap(b, bit)) for a, b in zip(have[:keep], have[keep:])]
        return have[0]

    def swap_halves(x, axis):
        low = lax.slice_in_dim(x, 0, half, axis=axis)
        high = lax.slice_in_dim(x, half, 2 * half, axis=axis)
        a = jnp.where(ci == 0, low, high)
        b = jnp.where(ci == 0, high, low)
        return jnp.concatenate([a, b], axis=axis)

    def columns(vector):
        count = -(-vector.size // shard)
        return jnp.pad(vector, (0, count * shard - vector.size)).reshape(count, shard).T

    own_vectors = swap_halves(
        jnp.stack([out_bias, gain_one, shift_one, gain_two, shift_two, down_bias]), 1
    )
    qv_rows = -(-qv // shard)
    own_bias = jnp.pad(qv_bias.reshape(1, qv), ((0, 0), (0, qv_rows * shard - qv))).reshape(qv_rows, shard)
    own_columns = on_chip(
        turn_kernel, [shaped((shard, round_up(6 + qv_rows, 8)), bf16)], [own_vectors, own_bias]
    )[0]
    wire_a = jnp.concatenate(
        [qkv_proj.reshape(shard, wide), out_proj.reshape(heads * HD, shard).T], axis=1
    )
    wire_a = jnp.concatenate([swap_halves(wire_a, 0), own_columns], axis=1)
    wires_a = gather_units(wire_a[None], far_bits)
    wire_b = swap_halves(jnp.concatenate([up_proj, down_proj.T], axis=1), 0)
    wire_b = jnp.concatenate([wire_b, columns(up_bias)], axis=1)
    near = len(fsdp_bits(0)) + 1
    gathered_a = gather_pieces(wires_a[0])

    lane = jnp.arange(feats, dtype=jnp.int32)
    part, at = lane // half_pad, lane % half_pad
    block = jnp.minimum(at // half, fsdp - 1) ^ fi
    source = jnp.where(at < used, block * shard + (part ^ ci) * half + at % half, -1)
    wire_b = add_after([wire_b[None]], gathered_a[0][near:])
    x = start(inputs, gi[None], source, rows, 0, wire_b)[0]
    wires_a += [tensor_swap(wires_a[0], pair_bit)]
    wires_a += [tensor_swap(add_after([w], [x]), pair_bit) for w in wires_a[1:-1]]
    wires_b = gather_units(wire_b, far_bits)
    gathered_b = [gather_pieces(wires_b[0])]
    found = start(cotangent, jnp.stack([gi, gi ^ 1]), source, rows, 1, gathered_b[0][0][1])
    cots, cots_t = found[:2], found[2:]
    out_share = jnp.arange(groups * share, dtype=jnp.int32)
    out_first = ((gi ^ (out_share // share)) * sub + ti % sub) * share + out_share % share
    pick = (out_first[:, None] == source[None, :half_pad]).astype(bf16)

    xn, xnt, vectors = first(x, *gathered_a, width, wide + heads * HD, [])
    kept, attn = attend(xn, *gathered_a, (0,), None, seq, heads, [cots[0]])
    later = on_chip(
        stack_kernel, [shaped((groups - 1,) + wire_a.shape, bf16)], wires_a[1:], after=gathered_b[0][0][near:]
    )[0]
    later = gather_pieces(later)
    held = [add_after([w], later[0][1:near]) for w in wires_b[1:]]
    gathered_b += [gather_pieces(w) for w in held]
    more, attn = attend(xn, *later, tuple(range(groups - 2)), attn, seq, heads, held)
    kept += more
    early = [a for g in gathered_b[1:] for a in g[0][1:near]]
    more, attn = attend(xn, *later, (groups - 2,), attn, seq, heads, early)
    kept += more

    def other_cores(parts):
        other = tensor_swap(parts, 1)
        for bit in core_bits[1:]:
            more = tensor_swap(jnp.stack([parts, other]), bit)
            parts, other = add_low(parts, more[0]), add_low(other, more[1])
        return parts, other

    attn, attn_other = other_cores(attn)
    middle, n2_low, n2_high = by_rows(
        functools.partial(middle_kernel, width),
        [shaped((rows, feats), f32), shaped((rows, half_pad), bf16), shaped((rows, half_pad), bf16)],
        [False] * 3,
        [x, attn, attn_other, vectors],
        [False, False, False, True],
        rows,
        tile,
        after=[a for g in gathered_b[1:] for a in g[0][1:near]],
    )
    far_low = tensor_swap(n2_low, pair_bit)

    out0, back0, up_bias0, dw0 = mlp(n2_low, n2_high, cots[0], cots_t[0], gathered_b, units, None)
    far_low = add_after([far_low], [up_bias0])
    far_high = tensor_swap(far_low, 1)
    out1, back1, up_bias_g, payload_b = mlp(
        far_low, far_high, cots[1], cots_t[1], gathered_b, units, list(dw0) + [up_bias0]
    )
    got_b = send(payload_b, 0)

    def other_half(parts):
        other = tensor_swap(parts[1], 1)
        for bit in core_bits[1:]:
            other = add_low(other, tensor_swap(add_low(parts[0], other), bit))
        return other

    def sum_cores(parts):
        return add_after([parts[0], other_half(parts)], [])

    back_far = tensor_swap(sum_cores(back1), pair_bit)
    back_low = add_low(sum_cores(back0), back_far)
    back_high = tensor_swap(back_low, 1)
    middle_grad, branch_grad, out_sum, sums2 = by_rows(
        functools.partial(middle_back_kernel, width),
        [
            shaped((rows, half_pad), f32),
            shaped((rows, feats), bf16),
            shaped((rows, half_pad), bf16),
            shaped((4, half_pad), f32),
        ],
        [False, False, False, True],
        [back_low, back_high, middle, cots[0], out1[0], other_half(out1), vectors],
        [False] * 6 + [True],
        rows,
        tile,
    )
    def spread(blocks):
        got = [blocks[:share]]
        for i in range(1, groups):
            got.append(tensor_swap(blocks[i * share : (i + 1) * share], i * sub))
        return got

    def collect(got):
        for i in range(len(group_bits)):
            swapped = [got[n ^ (1 << i)] for n in range(groups)]
            got = [jnp.where((gi >> i) & 1 == 1, s, g) for s, g in zip(swapped, got)]
        return jnp.stack([g.T[:seq] for g in got])

    stages = len(fsdp_bits(0))

    def rest_of(waiting, after):
        for stage in range(1, stages):
            waiting = fold(waiting, send(waiting, stage), stage, after)
        return waiting[0]

    middle_unit = groups // 2
    calls = [list(range(middle_unit, groups))[::-1]] + [[u] for u in range(middle_unit)[::-1]]
    back = None
    bias_calls = []
    payloads = []
    out_far = tensor_swap(out_sum, pair_bit)
    waiting_b = fold(payload_b, got_b, 0, [branch_grad])
    needed = [waiting_b[0]]
    for n, call in enumerate(calls):
        contexts = [kept[v][2] for u in call for v in (u, u - middle_unit)] if n == 0 else []
        payload, bias_g, back = attend_back(
            xnt, branch_grad, [kept[u] for u in call], contexts, back, seq, heads, half, needed
        )
        payloads.append(payload)
        bias_calls.append(bias_g)
        needed = []
        if n == 0:
            out_shares = by_rows_turned(
                out_kernel, [out0[0], other_half(out0), out_far, middle, back, vectors, pick], rows, tile, []
            )[0]
            out_got = spread(out_shares)
            layer_out = collect(out_got)
            grad_b = rest_of(waiting_b, [back])
            needed = [grad_b, out_shares]
        elif n == 1:
            waiting = fold(payloads[0], send(payloads[0], 0), 0, [back])
            needed = [waiting[0]] + out_got
    back_done = back
    back, back_other = other_cores(back)
    grad_b = scatter_units([grad_b[u] for u in range(len(wires_b))], far_bits, add_low)
    far = rest_of(waiting, [back_done])
    near_sums = [fold(p, send(p, 0), 0, [back_done]) for p in payloads[1:-1]]
    in_shares, sums1 = by_rows_turned(
        functools.partial(first_back_kernel, width),
        [back, back_other, x, middle_grad, far, vectors, pick],
        rows,
        tile,
        [(2, half_pad)],
    )
    in_got = spread(in_shares)
    last = fold(payloads[-1], send(payloads[-1], 0), 0, [in_shares])
    own = [rest_of(p, [in_shares])[0] for p in near_sums] + [rest_of(last, in_got)[0]]
    own = own[::-1]
    both = wide + heads * HD
    got = tensor_swap(far[..., :both], pair_bit)
    grads_a = []
    for u in range(middle_unit):
        n = calls[0].index(u + middle_unit)
        grads_a.append(add_low(jnp.concatenate([own[u], far[n, :, both:]], axis=1), got[n]))
    grad_a = scatter_units(grads_a, far_bits, add_low)
    grad_a, grad_o = grad_a[:, :wide], grad_a[:, wide:]
    input_grad = collect(in_got).astype(f32)

    small = on_chip(
        functools.partial(pack_kernel, heads, calls),
        [shaped((16, round_up(max(half_pad, qv, units), 128)), f32)],
        [sums1, sums2, up_bias_g] + bias_calls,
        after=[last[0]],
    )[0]
    rows_q, rows_b = groups, len(wires_b)
    for bit in (far_bits + [pair_bit])[::-1]:
        cut_b = bit != pair_bit
        small = on_chip(
            functools.partial(group_sum_kernel, groups, rows_q, rows_b, cut_b),
            [shaped(small.shape, f32)],
            [small, tensor_swap(small, bit)],
        )[0]
        rows_q //= 2
        rows_b = rows_b // 2 if cut_b else rows_b
    done_bits = []
    for bit in fsdp_bits(0):
        done_bits.append(bit)
        small = on_chip(
            functools.partial(block_sum_kernel, tuple(done_bits), half),
            [shaped(small.shape, f32)],
            [small, fsdp_swap(small, bit)],
        )[0]
    own_vector_g = small[:6, :half]
    vector_g = swap_halves(jnp.concatenate([own_vector_g, tensor_swap(own_vector_g, 1)], axis=1), 1)
    qvbias_g = small[6, :qv].reshape(heads, 2 * HD)
    upbias_g = small[6 + groups, :units]
    grad_a = swap_halves(grad_a.astype(f32), 0)
    grad_o = swap_halves(grad_o.astype(f32), 0)
    grad_b = swap_halves(grad_b.astype(f32), 0)
    return (
        layer_out,
        input_grad,
        grad_a.reshape(shard, heads, 3 * HD),
        qvbias_g,
        grad_o.T.reshape(heads, HD, shard),
        vector_g[0],
        vector_g[1],
        vector_g[2],
        vector_g[3],
        vector_g[4],
        grad_b[:, :units],
        upbias_g,
        grad_b[:, units:].T,
        vector_g[5],
    )


def by_rows_turned(kernel, args, rows, tile, sums):
    wide = args[-1].shape[0]

    def spec(shape):
        if len(shape) == 3:
            return pl.BlockSpec((shape[0], tile, shape[2]), lambda i: (0, i, 0))
        return pl.BlockSpec((tile, shape[1]), lambda i: (i, 0))

    whole = lambda shape: pl.BlockSpec(shape, lambda i: (0, 0))
    return pl.pallas_call(
        kernel,
        grid=(rows // tile,),
        in_specs=[spec(a.shape) for a in args[:-3]]
        + [pl.BlockSpec(memory_space=pl.ANY)]
        + [whole(a.shape) for a in args[-2:]],
        out_specs=[pl.BlockSpec((wide, tile), lambda i: (0, i))] + [whole(shape) for shape in sums],
        out_shape=[shaped((wide, rows), bf16)] + [shaped(shape, f32) for shape in sums],
        compiler_params=pltpu.CompilerParams(vmem_limit_bytes=16 * MIB),
        cost_estimate=pl.CostEstimate(
            flops=2 * rows * args[-1].size, bytes_accessed=12 * rows * args[0].shape[-1], transcendentals=0
        ),
    )(*args)


def solution(mesh):
    return jax.shard_map(
        body,
        mesh=mesh,
        in_specs=(
            P("fsdp", None, None),
            P("fsdp", None, None),
            P("fsdp", "tensor", None),
            P("tensor", None),
            P("tensor", None, "fsdp"),
            P("fsdp"),
            P("fsdp"),
            P("fsdp"),
            P("fsdp"),
            P("fsdp"),
            P("fsdp", "tensor"),
            P("tensor"),
            P("tensor", "fsdp"),
            P("fsdp"),
        ),
        out_specs=(
            P("fsdp", None, "tensor"),
            P("fsdp", None, "tensor"),
            P("fsdp", "tensor", None),
            P("tensor", None),
            P("tensor", None, "fsdp"),
            P("fsdp"),
            P("fsdp"),
            P("fsdp"),
            P("fsdp"),
            P("fsdp"),
            P("fsdp", "tensor"),
            P("tensor"),
            P("tensor", "fsdp"),
            P("fsdp"),
        ),
        check_vma=False,
    )
```
